512 devices in a mesh: dp: 128 (over x, y, z_lo, core), mp: 4 (over z_hi).
Axes of the slice: x: 4, y: 8, z: 8 (z_hi: 4, z_lo: 2; z = z_hi * 2 + z_lo), core: 2. Of those that a mesh axis runs over, the one named last changes fastest.
Arguments:
- patches: bfloat16 [256, 256, 1152], P('dp', None, 'mp'), may hold values from -6 to 6
- patch_count: int32 [256], P('dp'), may hold values from 1 to 256, as said below
- ln1_gain: float32 [1152], replicated, may hold values from 0.5 to 1.5
- w_qkv: bfloat16 [3, 1152, 1152], P(None, None, 'mp'), may hold values from -0.1875 to 0.1875
- w_out: bfloat16 [1152, 1152], P('mp'), may hold values from -0.1875 to 0.1875
- ln2_gain: float32 [1152], replicated, may hold values from 0.5 to 1.5
- pool_kv: bfloat16 [2, 1152, 1152], P(None, None, 'mp'), may hold values from -0.1875 to 0.1875
- pool_query: bfloat16 [1152], P('mp'), may hold values from -5 to 5
- pool_out: bfloat16 [1152, 1152], P('mp'), may hold values from -0.1875 to 0.1875
- text_emb: bfloat16 [256, 1152], P('dp'), may hold values from -6 to 6
- image_pair: int32 [256], P('dp'), may hold values from 0 to 255, each once
- logit_scale: float32 [], replicated, may hold values from 2 to 2.5
- logit_bias: float32 [], replicated, may hold values from -5 to -2.5
Outputs:
- image_grad: float32 [256, 1152], P('dp')
- text_grad: float32 [256, 1152], P('dp')
The draws below stay inside these ranges and needn't reach their ends.
Inputs may be any that keep to these rules, and one draw needn't show every extreme that they name: `patch_count`: each count is the product of an image grid's two sides, each 1 to 16; some image of every draw fills all 256 positions. `image_pair`: every text is the pair of exactly one image.
All inputs are finite; a program needn't handle non-finite values.
Results may differ from the reference program's by a relative error of at most 0.014.
Values may be sent and summed in bfloat16 or wider, within the bound.
No kernel may reach another device: no remote copies, remote signals or barrier semaphores. Data moves between devices by JAX's collectives and lax.ppermute only.
A program may use at most 64 MiB of HBM per device.

```python
import math
import jax
import jax.numpy as jnp
from jax import lax

D = 1152
HEADS = 16
HDIM = 72
SIDE = 16
PMAX = 256
IMAGES = 256


def draw_patch_count(key, part):
    key = jax.random.fold_in(key, 11)
    key_tall, key_wide = jax.random.split(key)
    tall_side = jax.random.randint(key_tall, (IMAGES,), 1, SIDE + 1)
    wide_side = jax.random.randint(key_wide, (IMAGES,), 1, SIDE + 1)
    counts = tall_side * wide_side
    return counts.at[0].set(SIDE * SIDE).astype(jnp.int32)


def block_scale(stream_key, shape, pieces, low, top_value):
    factor_of = 1.0
    for position, parts in pieces:
        draws = jax.random.uniform(jax.random.fold_in(jax.random.fold_in(stream_key, 6), position), (parts,), jnp.float32, low / len(pieces), top_value / len(pieces))
        factor_of = factor_of * jnp.repeat(jnp.exp(draws), shape[position] // parts).reshape((-1,) + (1,) * (len(shape) - 1 - position))
    return factor_of


def noise(key, extent, scale, bound, cuts=(), kind=jnp.bfloat16):
    factor_of = block_scale(key, extent, cuts, -0.22, 0.18) if cuts else 1.0
    entries = jax.random.normal(key, extent, jnp.float32) * scale * factor_of
    return jnp.minimum(jnp.maximum(entries, -bound), bound).astype(kind)


def setup_inputs(seed: int = 0) -> dict:
    seeds = jax.random.split(jax.random.key(seed), 14)
    return {
        "patches": noise(seeds[0], (IMAGES, PMAX, D), 1.0, 6.0, ((0, 128), (2, 4))),
        "patch_count": draw_patch_count(jax.random.fold_in(seeds[13], 71), 0),
        "ln1_gain": jnp.clip(1.0 + 0.1 * jax.random.normal(seeds[2], (D,), jnp.float32), 0.5, 1.5),
        "w_qkv": noise(seeds[3], (3, D, D), D ** -0.5, 0.1875, ((2, 4),)),
        "w_out": noise(seeds[4], (D, D), D ** -0.5, 0.1875, ((0, 4),)),
        "ln2_gain": jnp.clip(1.0 + 0.1 * jax.random.normal(seeds[5], (D,), jnp.float32), 0.5, 1.5),
        "pool_kv": noise(seeds[6], (2, D, D), D ** -0.5, 0.1875, ((2, 4),)),
        "pool_query": noise(seeds[7], (D,), 1.0, 5.0, ((0, 4),)),
        "pool_out": noise(seeds[8], (D, D), D ** -0.5, 0.1875, ((0, 4),)),
        "text_emb": noise(seeds[9], (IMAGES, D), 1.0, 6.0, ((0, 128),)),
        "image_pair": jax.random.permutation(seeds[10], IMAGES).astype(jnp.int32),
        "logit_scale": jnp.clip(jax.random.uniform(seeds[11], (), jnp.float32, 2.0, 2.5), 2.0, 2.5),
        "logit_bias": jnp.clip(jax.random.uniform(seeds[12], (), jnp.float32, -5.0, -2.5), -5.0, -2.5),
    }


def layer_norm(values, gain_vec):
    floats = values.astype(jnp.float32)
    center = floats - lax.optimization_barrier(jnp.mean(floats, axis=-1, keepdims=True))
    spread = lax.optimization_barrier(jnp.mean(center * center, axis=-1, keepdims=True))
    return center * lax.rsqrt(spread + 1e-06) * gain_vec

def masked_softmax(scores, valid_keys):
    scores = jnp.where(valid_keys, scores, -1e+30)
    highest = lax.optimization_barrier(jnp.max(scores, axis=-1, keepdims=True))
    raised = jnp.exp(scores - highest)
    return raised / lax.optimization_barrier(jnp.sum(raised, axis=-1, keepdims=True))

def reference(patches, patch_count, ln1_gain, w_qkv, w_out, ln2_gain, pool_kv, pool_query, pool_out, text_emb, image_pair, logit_scale, logit_bias):
    f32 = jnp.float32

    def embed_one(item):
        patch_one, count_one = item
        valid_keys = jnp.arange(PMAX, dtype=jnp.int32) < count_one
        normed = layer_norm(patch_one, ln1_gain).astype(jnp.bfloat16)
        proj = jnp.einsum('pd,cde->cpe', normed.astype(f32), w_qkv.astype(f32)).astype(jnp.bfloat16)
        proj = proj.reshape(3, PMAX, HEADS, HDIM).astype(f32)
        scores = jnp.einsum('qhe,khe->hqk', proj[0], proj[1]) / math.sqrt(HDIM)
        attn = masked_softmax(scores, valid_keys[None, None, :]).astype(jnp.bfloat16)
        context = jnp.einsum('hqk,khe->qhe', attn.astype(f32), proj[2]).astype(jnp.bfloat16).reshape(PMAX, D)
        stream = (patch_one.astype(f32) + jnp.dot(context, w_out, preferred_element_type=f32)).astype(jnp.bfloat16)
        normed2 = layer_norm(stream, ln2_gain).astype(jnp.bfloat16)
        keyval = jnp.einsum('pd,cde->cpe', normed2.astype(f32), pool_kv.astype(f32)).astype(jnp.bfloat16)
        keyval = keyval.reshape(2, PMAX, HEADS, HDIM).astype(f32)
        query = pool_query.astype(f32).reshape(HEADS, HDIM)
        pool_scores = jnp.einsum('he,phe->hp', query, keyval[0]) / math.sqrt(HDIM)
        pool_attn = masked_softmax(pool_scores, valid_keys[None, :]).astype(jnp.bfloat16)
        pooled = jnp.einsum('hp,phe->he', pool_attn.astype(f32), keyval[1]).astype(jnp.bfloat16).reshape(1, D)
        return jnp.dot(pooled, pool_out, preferred_element_type=f32)[0]
    embeds = lax.map(embed_one, (patches, patch_count))
    inv_img = lax.rsqrt(lax.optimization_barrier(jnp.sum(embeds * embeds, axis=-1, keepdims=True)) + 1e-06)
    zimg = embeds * inv_img
    texts = text_emb.astype(f32)
    inv_txt = lax.rsqrt(lax.optimization_barrier(jnp.sum(texts * texts, axis=-1, keepdims=True)) + 1e-06)
    ztxt = texts * inv_txt
    scale = jnp.exp(logit_scale)
    high = lax.Precision.HIGHEST
    logits = scale * jnp.dot(zimg, ztxt.T, precision=high) + logit_bias
    label = jnp.where(image_pair[:, None] == jnp.arange(IMAGES, dtype=jnp.int32)[None, :], 1.0, -1.0).astype(f32)
    dlog = -label * jax.nn.sigmoid(-label * logits)
    gimg = scale * jnp.dot(dlog, ztxt, precision=high)
    gtxt = scale * jnp.dot(dlog.T, zimg, precision=high)
    image_grad = (gimg - zimg * lax.optimization_barrier(jnp.sum(zimg * gimg, axis=-1, keepdims=True))) * inv_img
    text_grad = (gtxt - ztxt * lax.optimization_barrier(jnp.sum(ztxt * gtxt, axis=-1, keepdims=True))) * inv_txt
    return (image_grad, text_grad)
```

```python
import math

import jax
import jax.numpy as jnp
from jax import lax
from jax.sharding import PartitionSpec as P

HDIM = 72


def spread_all(value, axis):
    count = lax.axis_size(axis)
    return lax.all_to_all(jnp.broadcast_to(value[None], (count,) + value.shape), axis, 0, 0)


def layer_norm(values, gain_vec):
    floats = values.astype(jnp.float32)
    center = floats - jnp.mean(floats, axis=-1, keepdims=True)
    spread = jnp.mean(center * center, axis=-1, keepdims=True)
    return center * lax.rsqrt(spread + 1e-06) * gain_vec


def masked_softmax(scores, valid_keys):
    scores = jnp.where(valid_keys, scores, -1e30)
    highest = jnp.max(scores, axis=-1, keepdims=True)
    raised = jnp.exp(scores - highest)
    return raised / jnp.sum(raised, axis=-1, keepdims=True)


def split_bf16(values, terms):
    pieces = []
    for _ in range(terms):
        top = values.astype(jnp.bfloat16)
        pieces.append(top)
        values = values - top.astype(jnp.float32)
    return pieces


def per_device(
    patches,
    patch_count,
    ln1_gain,
    w_qkv,
    w_out,
    ln2_gain,
    pool_kv,
    pool_query,
    pool_out,
    text_emb,
    image_pair,
    logit_scale,
    logit_bias,
):
    f32, bf16 = jnp.float32, jnp.bfloat16
    rows_img, pmax, dlocal = patches.shape
    width = w_out.shape[1]
    local_heads = dlocal // HDIM
    heads = width // HDIM
    shards = lax.axis_size("mp")
    me = lax.axis_index("mp")
    rank = lax.axis_index("dp")
    half = pmax // 2
    nt = (((1,), (1,)), ((), ()))

    def dot(left, right, dims=(((1,), (0,)), ((), ()))):
        return lax.dot_general(left, right, dims, preferred_element_type=f32)

    def dot_exact(left, right, dims=(((1,), (0,)), ((), ()))):
        rows = left.shape[0]
        product = dot(jnp.concatenate(split_bf16(left, 3), axis=0), right, dims)
        return product[:rows] + product[rows : 2 * rows] + product[2 * rows :]

    tall = lax.all_gather(patches.transpose(0, 2, 1), "mp")

    texts_pairs = jnp.concatenate(
        [text_emb, jnp.broadcast_to(image_pair.astype(bf16)[:, None], (rows_img, 128))], axis=1
    )
    texts_pairs = spread_all(texts_pairs, "dp").reshape(-1, width + 128)
    text_all, pair_all = texts_pairs[:, :width], texts_pairs[:, width].astype(jnp.int32)
    texts = text_all.astype(f32)
    inv_txt = lax.rsqrt(jnp.sum(texts * texts, axis=-1) + 1e-06)

    head_of = jnp.arange(dlocal, dtype=jnp.int32) // HDIM
    own_head = head_of[None, :] == jnp.arange(local_heads, dtype=jnp.int32)[:, None]
    probe = jnp.where(own_head, pool_query[None, :], 0).astype(bf16)
    probe_keys = dot(probe, pool_kv[0], nt) * (1.0 / math.sqrt(HDIM))
    probe_all = spread_all(jnp.stack(split_bf16(probe_keys, 2)), "mp")
    probe_all = probe_all.transpose(1, 0, 2, 3).reshape(2 * heads, width)

    w_rows = w_qkv.transpose(0, 2, 1).reshape(3 * dlocal, width)
    blocks = []
    for i in range(rows_img):
        floats = tall[:, i].reshape(width, pmax).astype(f32)
        center = floats - jnp.mean(floats, axis=0, keepdims=True)
        spread = jnp.mean(center * center, axis=0, keepdims=True)
        normed = (center * lax.rsqrt(spread + 1e-06) * ln1_gain[:, None]).astype(bf16)
        proj = dot(w_rows, normed).astype(bf16).reshape(3, local_heads, HDIM, pmax)
        valid_keys = jnp.arange(pmax, dtype=jnp.int32) < patch_count[i]
        scores = jnp.einsum("heq,hek->hqk", proj[0], proj[1], preferred_element_type=f32) / math.sqrt(HDIM)
        attn = masked_softmax(scores, valid_keys[None, None, :]).astype(bf16)
        context = jnp.einsum("hek,hqk->heq", proj[2], attn, preferred_element_type=f32).astype(bf16)
        context = context.reshape(dlocal, pmax)
        partial = lax.dot_general(context, w_out, (((0,), (0,)), ((), ())), preferred_element_type=f32)
        blocks.append(partial.astype(bf16).reshape(2, half, width))

    parts = lax.all_to_all(jnp.concatenate(blocks, axis=0), "mp", 0, 0)
    my_image, my_half = me // 2, me % 2
    mine = jnp.where(my_image == 0, tall[:, 0], tall[:, 1]).reshape(width, pmax)
    resid = jnp.where(my_half == 0, mine[:, :half], mine[:, half:]).T
    stream = (resid.astype(f32) + jnp.sum(parts.astype(f32), axis=0)).astype(bf16)
    normed2 = layer_norm(stream, ln2_gain).astype(bf16)
    both = dot(probe_all, normed2, nt)
    pool_scores = both[:heads] + both[heads:]
    row_ids = my_half * half + jnp.arange(half, dtype=jnp.int32)
    my_count = jnp.where(my_image == 0, patch_count[0], patch_count[1])
    pool_scores = jnp.where((row_ids < my_count)[None, :], pool_scores, -1e30)
    highest = jnp.max(pool_scores, axis=-1, keepdims=True)
    raised = jnp.exp(pool_scores - highest)
    total = jnp.sum(raised, axis=-1, keepdims=True)
    mixed = dot((raised / total).astype(bf16), normed2)
    lse = jnp.broadcast_to(highest + jnp.log(total), (heads, 128))
    send = jnp.concatenate([mixed, lse], axis=1).reshape(shards, local_heads, width + 128)
    halves = lax.all_to_all(send, "mp", 0, 0).reshape(rows_img, 2, local_heads, width + 128)
    lse_all = halves[..., width : width + 1]
    share = jnp.exp(lse_all - jnp.max(lse_all, axis=1, keepdims=True))
    share = share / jnp.sum(share, axis=1, keepdims=True)
    mixed = jnp.sum(share * halves[..., :width], axis=1).reshape(rows_img * local_heads, width)
    vals = dot_exact(mixed, pool_kv[1]).reshape(rows_img, local_heads, dlocal)
    pooled = jnp.sum(jnp.where(own_head[None], vals, 0.0), axis=1).astype(bf16)
    embeds = lax.psum(dot(pooled, pool_out), "mp")

    inv_img_own = lax.rsqrt(jnp.sum(embeds * embeds, axis=-1, keepdims=True) + 1e-06)
    zimg_own = embeds * inv_img_own
    zimg = spread_all(zimg_own.astype(bf16), "dp").reshape(-1, width)

    scale = jnp.exp(logit_scale)
    first = rank * rows_img
    own_ids = first + jnp.arange(rows_img, dtype=jnp.int32)
    every = jnp.arange(zimg.shape[0], dtype=jnp.int32)
    text_own = text_emb.astype(f32)
    inv_txt_own = lax.rsqrt(jnp.sum(text_own * text_own, axis=-1, keepdims=True) + 1e-06)
    ztxt_own = text_own * inv_txt_own

    def slope(logits, is_pair):
        label = jnp.where(is_pair, 1.0, -1.0).astype(f32)
        return -label * jax.nn.sigmoid(-label * logits)

    logits_img = scale * dot_exact(zimg_own, text_all, nt) * inv_txt[None, :] + logit_bias
    dlog_img = slope(logits_img, image_pair[:, None] == every[None, :])
    logits_txt = scale * dot(text_emb, zimg, nt) * inv_txt_own + logit_bias
    dlog_txt = slope(logits_txt, pair_all[None, :] == own_ids[:, None])
    gimg = scale * dot_exact(dlog_img * inv_txt[None, :], text_all)
    gtxt = scale * dot_exact(dlog_txt, zimg)
    image_grad = (gimg - zimg_own * jnp.sum(zimg_own * gimg, axis=-1, keepdims=True)) * inv_img_own
    text_grad = (gtxt - ztxt_own * jnp.sum(ztxt_own * gtxt, axis=-1, keepdims=True)) * inv_txt_own
    return (image_grad, text_grad)


def solution(mesh):
    placed = (
        P("dp", None, "mp"),
        P("dp"),
        P(),
        P(None, None, "mp"),
        P("mp", None),
        P(),
        P(None, None, "mp"),
        P("mp"),
        P("mp", None),
        P("dp", None),
        P("dp"),
        P(),
        P(),
    )
    return jax.shard_map(
        per_device,
        mesh=mesh,
        in_specs=placed,
        out_specs=(P("dp", None), P("dp", None)),
        check_vma=False,
    )
```

```python
import math

import jax
import jax.numpy as jnp
from jax import lax
from jax.experimental import pallas as pl
from jax.experimental.pallas import tpu as pltpu
from jax.sharding import PartitionSpec as P

HDIM = 72


def spread_all(value, axis):
    count = lax.axis_size(axis)
    return lax.all_to_all(jnp.broadcast_to(value[None], (count,) + value.shape), axis, 0, 0)


def shift(value, steps):
    count = lax.axis_size("mp")
    pairs = [(source, (source + steps) % count) for source in range(count)]
    return lax.ppermute(value, "mp", pairs)


def layer_norm(values, gain_vec):
    floats = values.astype(jnp.float32)
    center = floats - jnp.mean(floats, axis=-1, keepdims=True)
    spread = jnp.mean(center * center, axis=-1, keepdims=True)
    return center * lax.rsqrt(spread + 1e-06) * gain_vec


def split_bf16(values, terms):
    pieces = []
    for _ in range(terms):
        top = values.astype(jnp.bfloat16)
        pieces.append(top)
        values = values - top.astype(jnp.float32)
    return pieces


def matmul(left, right, dims=(((1,), (0,)), ((), ()))):
    return lax.dot_general(left, right, dims, preferred_element_type=jnp.float32)


NT = (((1,), (1,)), ((), ()))


def attend_kernel(count_ref, x_ref, w_ref, out_w_ref, gain_ref, o_ref, ctx_ref):
    f32, bf16 = jnp.float32, jnp.bfloat16
    shards, dlocal, pmax = x_ref.shape
    width = shards * dlocal
    count = count_ref[0]
    floats = x_ref[...].reshape(width, pmax).astype(f32)
    center = floats - jnp.sum(floats, axis=0, keepdims=True) * (1.0 / width)
    spread = jnp.sum(center * center, axis=0, keepdims=True) * (1.0 / width)
    normed = (center * lax.rsqrt(spread + 1e-06) * gain_ref[...]).astype(bf16)
    proj = matmul(w_ref[...], normed)
    live = lax.broadcasted_iota(jnp.int32, (pmax, pmax), 0) < count
    for h in range(dlocal // HDIM):
        q, k, v = (proj[c * dlocal + h * HDIM : c * dlocal + (h + 1) * HDIM] for c in range(3))
        scores = matmul(k.T.astype(bf16), q.astype(bf16)) * (1.0 / math.sqrt(HDIM))
        scores = jnp.where(live, scores, -1e30)
        raised = jnp.exp(scores - jnp.max(scores, axis=0, keepdims=True))
        total = jnp.sum(raised, axis=0, keepdims=True)
        ctx_ref[h * HDIM : (h + 1) * HDIM] = matmul(v.astype(bf16), raised.astype(bf16)) / total
    context = ctx_ref[...].T.astype(bf16)
    o_ref[...] = matmul(context, out_w_ref[...]).astype(bf16)


def attend(count, slices, w_rows, w_out, gain):
    shards, dlocal, pmax = slices.shape
    width = w_rows.shape[1]
    flops = 2 * pmax * (3 * dlocal * width + 2 * dlocal * pmax + dlocal * width)
    return pl.pallas_call(
        attend_kernel,
        in_specs=[pl.BlockSpec(memory_space=pltpu.SMEM)] + [pl.BlockSpec(memory_space=pltpu.VMEM)] * 4,
        out_specs=pl.BlockSpec(memory_space=pltpu.VMEM),
        out_shape=jax.ShapeDtypeStruct((pmax, width), jnp.bfloat16),
        scratch_shapes=[pltpu.VMEM((dlocal, pmax), jnp.float32)],
        compiler_params=pltpu.CompilerParams(vmem_limit_bytes=40 * 1024 * 1024),
        cost_estimate=pl.CostEstimate(
            flops=flops, bytes_accessed=8 * width * dlocal + 4 * pmax * width, transcendentals=0
        ),
        name="attend",
    )(count.reshape(1), slices, w_rows, w_out, gain)


def pool_kernel(halves_ref, val_ref, out_w_ref, o_ref):
    f32, bf16 = jnp.float32, jnp.bfloat16
    dlocal, width = out_w_ref.shape
    heads = dlocal // HDIM
    images = halves_ref.shape[0] // (2 * heads)
    mixed = []
    for i in range(images):
        first = halves_ref[2 * i * heads : (2 * i + 1) * heads]
        second = halves_ref[(2 * i + 1) * heads : (2 * i + 2) * heads]
        lse_a, lse_b = first[:, width : width + 1], second[:, width : width + 1]
        top = jnp.maximum(lse_a, lse_b)
        raised_a, raised_b = jnp.exp(lse_a - top), jnp.exp(lse_b - top)
        total = raised_a + raised_b
        mixed.append(first[:, :width] * (raised_a / total) + second[:, :width] * (raised_b / total))
    mixed = jnp.concatenate(mixed, axis=0)
    rows = images * heads
    terms = []
    for _ in range(2):
        top = mixed.astype(bf16).astype(f32)
        terms.append(top)
        mixed = mixed - top
    vals = matmul(jnp.concatenate(terms, axis=0).astype(bf16), val_ref[0], NT)
    vals = vals[:rows] + vals[rows:]
    row = lax.broadcasted_iota(jnp.int32, (rows, dlocal), 0)
    lane = lax.broadcasted_iota(jnp.int32, (rows, dlocal), 1)
    start = (row % heads) * HDIM
    vals = jnp.where((lane >= start) & (lane < start + HDIM), vals, 0.0)
    pooled = [jnp.sum(vals[i * heads : (i + 1) * heads], axis=0, keepdims=True) for i in range(images)]
    pooled.append(jnp.zeros((16 - images, dlocal), f32))
    pooled = jnp.concatenate(pooled, axis=0).astype(bf16)
    o_ref[...] = matmul(pooled, out_w_ref[...])[:images]


def pool_embed(halves, pool_kv_rows, pool_out):
    dlocal, width = pool_out.shape
    images = halves.shape[0] // (2 * (dlocal // HDIM))
    return pl.pallas_call(
        pool_kernel,
        grid=(1,),
        in_specs=[
            pl.BlockSpec(halves.shape, lambda i: (0, 0)),
            pl.BlockSpec((1, dlocal, width), lambda i: (1, 0, 0)),
            pl.BlockSpec((dlocal, width), lambda i: (0, 0)),
        ],
        out_specs=pl.BlockSpec((images, width), lambda i: (0, 0)),
        out_shape=jax.ShapeDtypeStruct((images, width), jnp.float32),
        compiler_params=pltpu.CompilerParams(vmem_limit_bytes=24 * 1024 * 1024),
        name="pool_embed",
    )(halves, pool_kv_rows, pool_out)


def per_device(
    patches,
    patch_count,
    ln1_gain,
    w_qkv,
    w_out,
    ln2_gain,
    pool_kv,
    pool_query,
    pool_out,
    text_emb,
    image_pair,
    logit_scale,
    logit_bias,
):
    f32, bf16 = jnp.float32, jnp.bfloat16
    rows_img, pmax, dlocal = patches.shape
    width = w_out.shape[1]
    local_heads = dlocal // HDIM
    heads = width // HDIM
    shards = lax.axis_size("mp")
    me = lax.axis_index("mp")
    rank = lax.axis_index(("plane", "near"))
    half = pmax // 2
    nt = (((1,), (1,)), ((), ()))

    def dot(left, right, dims=(((1,), (0,)), ((), ()))):
        return lax.dot_general(left, right, dims, preferred_element_type=f32)

    def dot_exact(left, right, dims=(((1,), (0,)), ((), ()))):
        rows = left.shape[0]
        product = dot(jnp.concatenate(split_bf16(left, 3), axis=0), right, dims)
        return product[:rows] + product[rows : 2 * rows] + product[2 * rows :]

    my_image, my_half = me // 2, me % 2
    tall = patches.transpose(0, 2, 1)
    x_other = lax.all_to_all(jnp.stack([tall[1 - d // 2] for d in range(shards)]), "mp", 0, 0)
    x_mine = lax.all_to_all(jnp.stack([tall[d // 2] for d in range(shards)]), "mp", 0, 0)

    texts_pairs = jnp.concatenate(
        [text_emb, jnp.broadcast_to(image_pair.astype(bf16)[:, None], (rows_img, 128))], axis=1
    )
    texts_pairs, x_other = lax.optimization_barrier((texts_pairs, x_other))
    texts_pairs = spread_all(texts_pairs, ("plane", "near")).reshape(-1, width + 128)
    text_all, pair_all = texts_pairs[:, :width], texts_pairs[:, width].astype(jnp.int32)
    texts = text_all.astype(f32)
    inv_txt = lax.rsqrt(jnp.sum(texts * texts, axis=-1) + 1e-06)

    head_of = jnp.arange(dlocal, dtype=jnp.int32) // HDIM
    own_head = head_of[None, :] == jnp.arange(local_heads, dtype=jnp.int32)[:, None]
    probe = jnp.where(own_head, pool_query[None, :], 0).astype(bf16)
    probe_keys = dot(probe, pool_kv[0], nt) * (1.0 / math.sqrt(HDIM))
    probe_all = spread_all(jnp.stack(split_bf16(probe_keys, 2)), "mp")
    probe_all = probe_all.transpose(1, 0, 2, 3).reshape(2 * heads, width)

    w_rows = w_qkv.transpose(0, 2, 1).reshape(3 * dlocal, width)
    gain = ln1_gain[:, None]
    my_count = jnp.where(my_image == 0, patch_count[0], patch_count[1])
    other_count = jnp.where(my_image == 0, patch_count[1], patch_count[0])
    first = attend(other_count, x_other, w_rows, w_out, gain)
    second = attend(my_count, x_mine, w_rows, w_out, gain)

    quarter = half // 2
    far = lax.dynamic_slice(first, (my_half * half, 0), (half, width))
    far_after, far_before = shift(far[:quarter], 1), shift(far[quarter:], -1)
    even = my_half == 0
    after = jnp.where(even, second[half:], first[:half])
    before = jnp.where(even, first[half:], second[:half])
    own_part = jnp.where(even, second[:half], second[half:]).astype(f32)

    def added(left, right):
        return (left.astype(f32) + right.astype(f32)).astype(bf16)

    after = jnp.concatenate([added(after[:quarter], far_after), after[quarter:]], axis=0)
    before = jnp.concatenate([before[:quarter], added(before[quarter:], far_before)], axis=0)
    parts = own_part + shift(after, 1).astype(f32) + shift(before, -1).astype(f32)
    mine = x_mine.reshape(width, pmax)
    resid = jnp.where(my_half == 0, mine[:, :half], mine[:, half:]).T
    stream = (resid.astype(f32) + parts).astype(bf16)
    normed2 = layer_norm(stream, ln2_gain).astype(bf16)
    both = dot(probe_all, normed2, nt)
    pool_scores = both[:heads] + both[heads:]
    row_ids = my_half * half + jnp.arange(half, dtype=jnp.int32)
    pool_scores = jnp.where((row_ids < my_count)[None, :], pool_scores, -1e30)
    highest = jnp.max(pool_scores, axis=-1, keepdims=True)
    raised = jnp.exp(pool_scores - highest)
    total = jnp.sum(raised, axis=-1, keepdims=True)
    mixed = dot((raised / total).astype(bf16), normed2)
    lse = jnp.broadcast_to(highest + jnp.log(total), (heads, 128))
    send = jnp.concatenate([mixed, lse], axis=1).reshape(shards, local_heads, width + 128)
    halves = lax.all_to_all(send, "mp", 0, 0).reshape(shards * local_heads, width + 128)
    shares = pool_embed(halves, pool_kv.transpose(0, 2, 1), pool_out)

    shares = spread_all(shares, ("near", "mp"))
    embeds = jnp.sum(shares.reshape(-1, shards, rows_img, width), axis=1).reshape(-1, width)
    inv_img = lax.rsqrt(jnp.sum(embeds * embeds, axis=-1, keepdims=True) + 1e-06)
    zimg_near = embeds * inv_img
    start = lax.axis_index("near") * rows_img
    zimg_own = lax.dynamic_slice(zimg_near, (start, 0), (rows_img, width))
    inv_img_own = lax.dynamic_slice(inv_img, (start, 0), (rows_img, 1))
    zimg = spread_all(zimg_near.astype(bf16), "plane").reshape(-1, width)

    scale = jnp.exp(logit_scale)
    own_ids = rank * rows_img + jnp.arange(rows_img, dtype=jnp.int32)
    every = jnp.arange(zimg.shape[0], dtype=jnp.int32)
    text_own = text_emb.astype(f32)
    inv_txt_own = lax.rsqrt(jnp.sum(text_own * text_own, axis=-1, keepdims=True) + 1e-06)
    ztxt_own = text_own * inv_txt_own

    def slope(logits, is_pair):
        label = jnp.where(is_pair, 1.0, -1.0).astype(f32)
        return -label * jax.nn.sigmoid(-label * logits)

    logits_img = scale * dot_exact(zimg_own, text_all, nt) * inv_txt[None, :] + logit_bias
    dlog_img = slope(logits_img, image_pair[:, None] == every[None, :])
    logits_txt = scale * dot(text_emb, zimg, nt) * inv_txt_own + logit_bias
    dlog_txt = slope(logits_txt, pair_all[None, :] == own_ids[:, None])
    gimg = scale * dot_exact(dlog_img * inv_txt[None, :], text_all)
    gtxt = scale * dot_exact(dlog_txt, zimg)
    image_grad = (gimg - zimg_own * jnp.sum(zimg_own * gimg, axis=-1, keepdims=True)) * inv_img_own
    text_grad = (gtxt - ztxt_own * jnp.sum(ztxt_own * gtxt, axis=-1, keepdims=True)) * inv_txt_own
    return (image_grad, text_grad)


def solution(mesh):
    shards = mesh.shape["mp"]
    devices = mesh.devices.reshape(-1, 4, shards)
    fine = jax.sharding.Mesh(devices, ("plane", "near", "mp"))
    dp = ("plane", "near")
    placed = (
        P(dp, None, "mp"),
        P(dp),
        P(),
        P(None, None, "mp"),
        P("mp", None),
        P(),
        P(None, None, "mp"),
        P("mp"),
        P("mp", None),
        P(dp, None),
        P(dp),
        P(),
        P(),
    )
    return jax.shard_map(
        per_device,
        mesh=fine,
        in_specs=placed,
        out_specs=(P(dp, None), P(dp, None)),
        check_vma=False,
    )
```

```python
import math

import jax
import jax.numpy as jnp
from jax import lax
from jax.experimental import pallas as pl
from jax.experimental.pallas import tpu as pltpu
from jax.sharding import PartitionSpec as P

HDIM = 72


def spread_all(value, axis):
    count = lax.axis_size(axis)
    return lax.all_to_all(jnp.broadcast_to(value[None], (count,) + value.shape), axis, 0, 0)


def shift(value, steps):
    count = lax.axis_size("mp")
    pairs = [(source, (source + steps) % count) for source in range(count)]
    return lax.ppermute(value, "mp", pairs)


def layer_norm(values, gain_vec):
    floats = values.astype(jnp.float32)
    center = floats - jnp.mean(floats, axis=-1, keepdims=True)
    spread = jnp.mean(center * center, axis=-1, keepdims=True)
    return center * lax.rsqrt(spread + 1e-06) * gain_vec


def split_bf16(values, terms):
    pieces = []
    for _ in range(terms):
        top = values.astype(jnp.bfloat16)
        pieces.append(top)
        values = values - top.astype(jnp.float32)
    return pieces


def matmul(left, right, dims=(((1,), (0,)), ((), ()))):
    return lax.dot_general(left, right, dims, preferred_element_type=jnp.float32)


NT = (((1,), (1,)), ((), ()))


def attend_kernel(scalar_ref, own_ref, left_ref, right_ref, far_a_ref, far_b_ref, w_ref, out_w_ref, gain_ref,
                  o_ref, x_ref, norm_ref, ctx_ref):
    f32, bf16 = jnp.float32, jnp.bfloat16
    width, pmax = x_ref.shape
    dlocal = out_w_ref.shape[0]
    shards = width // dlocal
    me, image, count = scalar_ref[0], scalar_ref[1], scalar_ref[2]
    far = jnp.where(image == 0, far_a_ref[...].astype(f32), far_b_ref[...].astype(f32))
    slices = [ref[...].astype(f32) for ref in (own_ref, left_ref, right_ref)] + [far]
    mean = sum(jnp.sum(part, axis=0, keepdims=True) for part in slices) * (1.0 / width)
    centers = [part - mean for part in slices]
    spread = sum(jnp.sum(part * part, axis=0, keepdims=True) for part in centers) * (1.0 / width)
    scale = lax.rsqrt(spread + 1e-06)
    for part, center, steps in zip(slices, centers, (0, shards - 1, 1, 2)):
        source = lax.rem(me + steps, shards)
        place = pl.ds(pl.multiple_of(source * dlocal, 16), dlocal)
        x_ref[place] = part.astype(bf16)
        norm_ref[place] = (center * scale * gain_ref[place]).astype(bf16)
    proj = matmul(w_ref[...], norm_ref[...])
    live = lax.broadcasted_iota(jnp.int32, (pmax, pmax), 0) < count
    for h in range(dlocal // HDIM):
        q, k, v = (proj[c * dlocal + h * HDIM : c * dlocal + (h + 1) * HDIM] for c in range(3))
        scores = matmul(k.T.astype(bf16), q.astype(bf16)) * (1.0 / math.sqrt(HDIM))
        scores = jnp.where(live, scores, -1e30)
        raised = jnp.exp(scores - jnp.max(scores, axis=0, keepdims=True))
        total = jnp.sum(raised, axis=0, keepdims=True)
        ctx_ref[h * HDIM : (h + 1) * HDIM] = matmul(v.astype(bf16), raised.astype(bf16)) / total
    context = ctx_ref[...].T.astype(bf16)
    o_ref[...] = matmul(context, out_w_ref[...]).astype(bf16)


def attend(scalars, slices, w_rows, w_out, gain):
    pmax = slices[0].shape[1]
    dlocal, width = w_out.shape
    flops = 2 * pmax * (3 * dlocal * width + 2 * dlocal * pmax + dlocal * width)
    of_image = pl.BlockSpec((dlocal, pmax), lambda i, scalar_ref: (scalar_ref[1], 0))
    whole = lambda *shape: pl.BlockSpec(shape, lambda i, scalar_ref: (0, 0))
    return pl.pallas_call(
        attend_kernel,
        grid_spec=pltpu.PrefetchScalarGridSpec(
            num_scalar_prefetch=1,
            grid=(1,),
            in_specs=[of_image] * 3
            + [whole(dlocal, pmax)] * 2
            + [whole(3 * dlocal, width), whole(dlocal, width), whole(width, 1)],
            out_specs=[whole(pmax, width), whole(width, pmax)],
            scratch_shapes=[pltpu.VMEM((width, pmax), jnp.bfloat16), pltpu.VMEM((dlocal, pmax), jnp.float32)],
        ),
        out_shape=[
            jax.ShapeDtypeStruct((pmax, width), jnp.bfloat16),
            jax.ShapeDtypeStruct((width, pmax), jnp.bfloat16),
        ],
        compiler_params=pltpu.CompilerParams(vmem_limit_bytes=32 * 1024 * 1024),
        cost_estimate=pl.CostEstimate(
            flops=flops, bytes_accessed=8 * width * dlocal + 8 * pmax * width, transcendentals=0
        ),
        name="attend",
    )(jnp.stack(scalars).astype(jnp.int32), *slices, w_rows, w_out, gain)


def pool_kernel(halves_ref, val_ref, out_w_ref, o_ref):
    f32, bf16 = jnp.float32, jnp.bfloat16
    dlocal, width = out_w_ref.shape
    heads = dlocal // HDIM
    images = halves_ref.shape[0] // (2 * heads)
    mixed = []
    for i in range(images):
        first = halves_ref[2 * i * heads : (2 * i + 1) * heads]
        second = halves_ref[(2 * i + 1) * heads : (2 * i + 2) * heads]
        lse_a, lse_b = first[:, width : width + 1], second[:, width : width + 1]
        top = jnp.maximum(lse_a, lse_b)
        raised_a, raised_b = jnp.exp(lse_a - top), jnp.exp(lse_b - top)
        total = raised_a + raised_b
        mixed.append(first[:, :width] * (raised_a / total) + second[:, :width] * (raised_b / total))
    mixed = jnp.concatenate(mixed, axis=0)
    rows = images * heads
    terms = []
    for _ in range(2):
        top = mixed.astype(bf16).astype(f32)
        terms.append(top)
        mixed = mixed - top
    vals = matmul(jnp.concatenate(terms, axis=0).astype(bf16), val_ref[0], NT)
    vals = vals[:rows] + vals[rows:]
    row = lax.broadcasted_iota(jnp.int32, (rows, dlocal), 0)
    lane = lax.broadcasted_iota(jnp.int32, (rows, dlocal), 1)
    start = (row % heads) * HDIM
    vals = jnp.where((lane >= start) & (lane < start + HDIM), vals, 0.0)
    pooled = [jnp.sum(vals[i * heads : (i + 1) * heads], axis=0, keepdims=True) for i in range(images)]
    pooled.append(jnp.zeros((16 - images, dlocal), f32))
    pooled = jnp.concatenate(pooled, axis=0).astype(bf16)
    o_ref[...] = matmul(pooled, out_w_ref[...])[:images]


def pool_embed(halves, pool_kv_rows, pool_out):
    dlocal, width = pool_out.shape
    images = halves.shape[0] // (2 * (dlocal // HDIM))
    return pl.pallas_call(
        pool_kernel,
        grid=(1,),
        in_specs=[
            pl.BlockSpec(halves.shape, lambda i: (0, 0)),
            pl.BlockSpec((1, dlocal, width), lambda i: (1, 0, 0)),
            pl.BlockSpec((dlocal, width), lambda i: (0, 0)),
        ],
        out_specs=pl.BlockSpec((images, width), lambda i: (0, 0)),
        out_shape=jax.ShapeDtypeStruct((images, width), jnp.float32),
        compiler_params=pltpu.CompilerParams(vmem_limit_bytes=12 * 1024 * 1024),
        name="pool_embed",
    )(halves, pool_kv_rows, pool_out)


def per_device(
    patches,
    patch_count,
    ln1_gain,
    w_qkv,
    w_out,
    ln2_gain,
    pool_kv,
    pool_query,
    pool_out,
    text_emb,
    image_pair,
    logit_scale,
    logit_bias,
):
    f32, bf16 = jnp.float32, jnp.bfloat16
    rows_img, pmax, dlocal = patches.shape
    width = w_out.shape[1]
    local_heads = dlocal // HDIM
    heads = width // HDIM
    shards = lax.axis_size("mp")
    me = lax.axis_index("mp")
    half = pmax // 2
    nt = (((1,), (1,)), ((), ()))

    def dot(left, right, dims=(((1,), (0,)), ((), ()))):
        return lax.dot_general(left, right, dims, preferred_element_type=f32)

    def dot_exact(left, right, dims=(((1,), (0,)), ((), ()))):
        rows = left.shape[0]
        product = dot(jnp.concatenate(split_bf16(left, 3), axis=0), right, dims)
        return product[:rows] + product[rows : 2 * rows] + product[2 * rows :]

    head_of = jnp.arange(dlocal, dtype=jnp.int32) // HDIM
    own_head = head_of[None, :] == jnp.arange(local_heads, dtype=jnp.int32)[:, None]
    probe = jnp.where(own_head, pool_query[None, :], 0).astype(bf16)
    probe_keys = dot(probe, pool_kv[0], nt) * (1.0 / math.sqrt(HDIM))
    probe_keys = jnp.concatenate(split_bf16(probe_keys, 2), axis=0).reshape(-1, pmax)
    probe_rows = probe_keys.shape[0]
    padding = jnp.zeros((-probe_rows % 16, pmax), bf16)

    own_x = jnp.concatenate([patches[0].T, patches[1].T, probe_keys, padding], axis=0)
    left_x, right_x = shift(own_x, 1), shift(own_x, -1)

    slot, side = me % 2, me // 2
    texts = spread_all(jnp.where(slot == 0, text_emb[0], text_emb[1])[None], "plane").reshape(-1, width)
    texts, left_x, right_x = lax.optimization_barrier((texts, left_x, right_x))
    far_a, far_b = shift(left_x[:dlocal], 1), shift(right_x[dlocal:], -1)
    came = [own_x[2 * dlocal :], right_x[2 * dlocal :], far_b[dlocal:], left_x[2 * dlocal :]]
    came = [x[:probe_rows] for x in came]
    probe_all = jnp.stack([lax.select_n((j - me) % shards, *came) for j in range(shards)])
    probe_all = probe_all.reshape(shards, 2, local_heads, width).transpose(1, 0, 2, 3).reshape(2 * heads, width)

    my_image, my_half = me // 2, me % 2
    w_rows = w_qkv.transpose(0, 2, 1).reshape(3 * dlocal, width)
    gain = ln1_gain[:, None]
    my_count = jnp.where(my_image == 0, patch_count[0], patch_count[1])
    other_count = jnp.where(my_image == 0, patch_count[1], patch_count[0])
    slices = (own_x, left_x, right_x, far_a, far_b)
    first, _ = attend((me, 1 - my_image, other_count), slices, w_rows, w_out, gain)
    second, mine = attend((me, my_image, my_count), slices, w_rows, w_out, gain)

    even = my_half == 0
    far = shift(jnp.where(even, first[:half], first[half:]), 1)
    after = jnp.where(even, second[half:], first[:half])
    before = jnp.where(even, first[half:], second[:half])
    own_part = jnp.where(even, second[:half], second[half:]).astype(f32)
    after = (after.astype(f32) + far.astype(f32)).astype(bf16)
    parts = own_part + shift(after, 1).astype(f32) + shift(before, -1).astype(f32)
    resid = jnp.where(my_half == 0, mine[:, :half], mine[:, half:]).T
    stream = (resid.astype(f32) + parts).astype(bf16)
    normed2 = layer_norm(stream, ln2_gain).astype(bf16)
    both = dot(probe_all, normed2, nt)
    pool_scores = both[:heads] + both[heads:]
    row_ids = my_half * half + jnp.arange(half, dtype=jnp.int32)
    pool_scores = jnp.where((row_ids < my_count)[None, :], pool_scores, -1e30)
    highest = jnp.max(pool_scores, axis=-1, keepdims=True)
    raised = jnp.exp(pool_scores - highest)
    total = jnp.sum(raised, axis=-1, keepdims=True)
    mixed = dot((raised / total).astype(bf16), normed2)
    lse = jnp.broadcast_to(highest + jnp.log(total), (heads, 128))
    send = jnp.concatenate([mixed, lse], axis=1).reshape(shards, local_heads, width + 128)
    halves = lax.all_to_all(send, "mp", 0, 0).reshape(shards * local_heads, width + 128)
    shares = pool_embed(halves, pool_kv.transpose(0, 2, 1), pool_out)


    pairs = jnp.broadcast_to(image_pair.astype(f32)[:, None], (rows_img, 128))
    column = spread_all(jnp.concatenate([shares, pairs], axis=1), ("near", "mp"))
    column = column.reshape(-1, shards, rows_img, width + 128)
    embeds = jnp.sum(column[..., :width], axis=1)
    inv_img = lax.rsqrt(jnp.sum(embeds * embeds, axis=-1, keepdims=True) + 1e-06)
    zimg = embeds * inv_img

    scale = jnp.exp(logit_scale)
    planes, nears = texts.shape[0], embeds.shape[0]
    near = lax.axis_index("near")
    z_part = jnp.where(side == 0, zimg[:, 0], zimg[:, 1])
    pair_part = jnp.where(side == 0, column[:, 0, 0, width], column[:, 0, 1, width])
    text_ids = (jnp.arange(planes, dtype=jnp.int32) * nears + near) * rows_img + slot
    texts_f32 = texts.astype(f32)
    inv_txt = lax.rsqrt(jnp.sum(texts_f32 * texts_f32, axis=-1) + 1e-06)
    logits = scale * dot_exact(z_part, texts, nt) * inv_txt[None, :] + logit_bias
    is_pair = pair_part.astype(jnp.int32)[:, None] == text_ids[None, :]
    label = jnp.where(is_pair, 1.0, -1.0).astype(f32)
    dlog = -label * jax.nn.sigmoid(-label * logits) * scale
    gimg = dot_exact(dlog * inv_txt[None, :], texts)
    gtxt = sum(dlog[n][:, None] * z_part[n][None, :] for n in range(nears))

    gtxt = jnp.sum(lax.all_to_all(gtxt, "plane", 0, 0, tiled=True), axis=0)
    both = jnp.stack([gimg, jnp.broadcast_to(gtxt[None], gimg.shape)], axis=1)
    both = jnp.broadcast_to(both[:, None], (nears, shards, 2, width)).reshape(-1, 2, width)
    both = lax.all_to_all(both, ("near", "mp"), 0, 0).reshape(nears, rows_img, 2, 2, width)
    gimg = jnp.sum(both[:, :, :, 0], axis=(0, 2))
    gtxt = jnp.sum(lax.dynamic_index_in_dim(both, near, 0, False)[:, :, 1], axis=0)

    zimg_own = lax.dynamic_index_in_dim(zimg, near, 0, False)
    inv_img_own = lax.dynamic_index_in_dim(inv_img, near, 0, False)
    text_own = text_emb.astype(f32)
    inv_txt_own = lax.rsqrt(jnp.sum(text_own * text_own, axis=-1, keepdims=True) + 1e-06)
    ztxt_own = text_own * inv_txt_own
    image_grad = (gimg - zimg_own * jnp.sum(zimg_own * gimg, axis=-1, keepdims=True)) * inv_img_own
    text_grad = (gtxt - ztxt_own * jnp.sum(ztxt_own * gtxt, axis=-1, keepdims=True)) * inv_txt_own
    return (image_grad, text_grad)


def solution(mesh):
    devices = mesh.devices.reshape(-1, 4, mesh.shape["mp"])
    fine = jax.sharding.Mesh(devices, ("plane", "near", "mp"))
    dp = ("plane", "near")
    placed = (
        P(dp, None, "mp"),
        P(dp),
        P(),
        P(None, None, "mp"),
        P("mp", None),
        P(),
        P(None, None, "mp"),
        P("mp"),
        P("mp", None),
        P(dp, None),
        P(dp),
        P(),
        P(),
    )
    return jax.shard_map(
        per_device,
        mesh=fine,
        in_specs=placed,
        out_specs=(P(dp, None), P(dp, None)),
        check_vma=False,
    )
```

```python
import math

import jax
import jax.numpy as jnp
from jax import lax
from jax.experimental import pallas as pl
from jax.experimental.pallas import tpu as pltpu
from jax.sharding import PartitionSpec as P

HDIM = 72


def spread_all(value, axis):
    count = lax.axis_size(axis)
    return lax.all_to_all(jnp.broadcast_to(value[None], (count,) + value.shape), axis, 0, 0)


def shift(value, steps, axis="mp"):
    count = lax.axis_size(axis)
    pairs = [(source, (source + steps) % count) for source in range(count)]
    return lax.ppermute(value, axis, pairs)


def layer_norm(values, gain_vec):
    floats = values.astype(jnp.float32)
    center = floats - jnp.mean(floats, axis=-1, keepdims=True)
    spread = jnp.mean(center * center, axis=-1, keepdims=True)
    return center * lax.rsqrt(spread + 1e-06) * gain_vec


def split_bf16(values, terms):
    pieces = []
    for _ in range(terms):
        top = values.astype(jnp.bfloat16)
        pieces.append(top)
        values = values - top.astype(jnp.float32)
    return pieces


def matmul(left, right, dims=(((1,), (0,)), ((), ()))):
    return lax.dot_general(left, right, dims, preferred_element_type=jnp.float32)


NT = (((1,), (1,)), ((), ()))


def attend_kernel(scalar_ref, own_ref, left_ref, right_ref, far_a_ref, far_b_ref, w_ref, out_w_ref, gain_ref,
                  o_ref, x_ref, norm_ref, ctx_ref):
    f32, bf16 = jnp.float32, jnp.bfloat16
    width, pmax = x_ref.shape
    dlocal = out_w_ref.shape[0]
    shards = width // dlocal
    me, image, count = scalar_ref[0], scalar_ref[1], scalar_ref[2]
    far = jnp.where(image == 0, far_a_ref[...].astype(f32), far_b_ref[...].astype(f32))
    slices = [ref[...].astype(f32) for ref in (own_ref, left_ref, right_ref)] + [far]
    mean = sum(jnp.sum(part, axis=0, keepdims=True) for part in slices) * (1.0 / width)
    centers = [part - mean for part in slices]
    spread = sum(jnp.sum(part * part, axis=0, keepdims=True) for part in centers) * (1.0 / width)
    scale = lax.rsqrt(spread + 1e-06)
    for part, center, steps in zip(slices, centers, (0, shards - 1, 1, 2)):
        source = lax.rem(me + steps, shards)
        place = pl.ds(pl.multiple_of(source * dlocal, 16), dlocal)
        x_ref[place] = part.astype(bf16)
        norm_ref[place] = (center * scale * gain_ref[place]).astype(bf16)
    proj = matmul(w_ref[...], norm_ref[...])
    live = lax.broadcasted_iota(jnp.int32, (pmax, pmax), 0) < count
    for h in range(dlocal // HDIM):
        q, k, v = (proj[c * dlocal + h * HDIM : c * dlocal + (h + 1) * HDIM] for c in range(3))
        scores = matmul(k.T.astype(bf16), q.astype(bf16)) * (1.0 / math.sqrt(HDIM))
        scores = jnp.where(live, scores, -1e30)
        raised = jnp.exp(scores - jnp.max(scores, axis=0, keepdims=True))
        total = jnp.sum(raised, axis=0, keepdims=True)
        ctx_ref[h * HDIM : (h + 1) * HDIM] = matmul(v.astype(bf16), raised.astype(bf16)) / total
    context = ctx_ref[...].T.astype(bf16)
    o_ref[...] = matmul(context, out_w_ref[...]).astype(bf16)


def attend(scalars, slices, w_rows, w_out, gain):
    pmax = slices[0].shape[1]
    dlocal, width = w_out.shape
    flops = 2 * pmax * (3 * dlocal * width + 2 * dlocal * pmax + dlocal * width)
    of_image = pl.BlockSpec((dlocal, pmax), lambda i, scalar_ref: (scalar_ref[1], 0))
    whole = lambda *shape: pl.BlockSpec(shape, lambda i, scalar_ref: (0, 0))
    return pl.pallas_call(
        attend_kernel,
        grid_spec=pltpu.PrefetchScalarGridSpec(
            num_scalar_prefetch=1,
            grid=(1,),
            in_specs=[of_image] * 3
            + [whole(dlocal, pmax)] * 2
            + [whole(3 * dlocal, width), whole(dlocal, width), whole(width, 1)],
            out_specs=[whole(pmax, width), whole(width, pmax)],
            scratch_shapes=[pltpu.VMEM((width, pmax), jnp.bfloat16), pltpu.VMEM((dlocal, pmax), jnp.float32)],
        ),
        out_shape=[
            jax.ShapeDtypeStruct((pmax, width), jnp.bfloat16),
            jax.ShapeDtypeStruct((width, pmax), jnp.bfloat16),
        ],
        compiler_params=pltpu.CompilerParams(vmem_limit_bytes=32 * 1024 * 1024),
        cost_estimate=pl.CostEstimate(
            flops=flops, bytes_accessed=8 * width * dlocal + 8 * pmax * width, transcendentals=0
        ),
        name="attend",
    )(jnp.stack(scalars).astype(jnp.int32), *slices, w_rows, w_out, gain)


def pool_kernel(halves_ref, val_ref, out_w_ref, o_ref):
    f32, bf16 = jnp.float32, jnp.bfloat16
    dlocal, width = out_w_ref.shape
    heads = dlocal // HDIM
    images = halves_ref.shape[0] // (2 * heads)
    mixed = []
    for i in range(images):
        first = halves_ref[2 * i * heads : (2 * i + 1) * heads]
        second = halves_ref[(2 * i + 1) * heads : (2 * i + 2) * heads]
        lse_a, lse_b = first[:, width : width + 1], second[:, width : width + 1]
        top = jnp.maximum(lse_a, lse_b)
        raised_a, raised_b = jnp.exp(lse_a - top), jnp.exp(lse_b - top)
        total = raised_a + raised_b
        mixed.append(first[:, :width] * (raised_a / total) + second[:, :width] * (raised_b / total))
    mixed = jnp.concatenate(mixed, axis=0)
    rows = images * heads
    terms = []
    for _ in range(2):
        top = mixed.astype(bf16).astype(f32)
        terms.append(top)
        mixed = mixed - top
    vals = matmul(jnp.concatenate(terms, axis=0).astype(bf16), val_ref[0], NT)
    vals = vals[:rows] + vals[rows:]
    row = lax.broadcasted_iota(jnp.int32, (rows, dlocal), 0)
    lane = lax.broadcasted_iota(jnp.int32, (rows, dlocal), 1)
    start = (row % heads) * HDIM
    vals = jnp.where((lane >= start) & (lane < start + HDIM), vals, 0.0)
    pooled = [jnp.sum(vals[i * heads : (i + 1) * heads], axis=0, keepdims=True) for i in range(images)]
    pooled.append(jnp.zeros((16 - images, dlocal), f32))
    pooled = jnp.concatenate(pooled, axis=0).astype(bf16)
    o_ref[...] = matmul(pooled, out_w_ref[...])[:images]


def pool_embed(halves, pool_kv_rows, pool_out):
    dlocal, width = pool_out.shape
    images = halves.shape[0] // (2 * (dlocal // HDIM))
    return pl.pallas_call(
        pool_kernel,
        grid=(1,),
        in_specs=[
            pl.BlockSpec(halves.shape, lambda i: (0, 0)),
            pl.BlockSpec((1, dlocal, width), lambda i: (1, 0, 0)),
            pl.BlockSpec((dlocal, width), lambda i: (0, 0)),
        ],
        out_specs=pl.BlockSpec((images, width), lambda i: (0, 0)),
        out_shape=jax.ShapeDtypeStruct((images, width), jnp.float32),
        compiler_params=pltpu.CompilerParams(vmem_limit_bytes=12 * 1024 * 1024),
        name="pool_embed",
    )(halves, pool_kv_rows, pool_out)


def per_device(
    patches,
    patch_count,
    ln1_gain,
    w_qkv,
    w_out,
    ln2_gain,
    pool_kv,
    pool_query,
    pool_out,
    text_emb,
    image_pair,
    logit_scale,
    logit_bias,
):
    f32, bf16 = jnp.float32, jnp.bfloat16
    rows_img, pmax, dlocal = patches.shape
    width = w_out.shape[1]
    local_heads = dlocal // HDIM
    heads = width // HDIM
    shards = lax.axis_size("mp")
    me = lax.axis_index("mp")
    half = pmax // 2
    nt = (((1,), (1,)), ((), ()))

    def dot(left, right, dims=(((1,), (0,)), ((), ()))):
        return lax.dot_general(left, right, dims, preferred_element_type=f32)

    def dot_exact(left, right, dims=(((1,), (0,)), ((), ()))):
        rows = left.shape[0]
        product = dot(jnp.concatenate(split_bf16(left, 3), axis=0), right, dims)
        return product[:rows] + product[rows : 2 * rows] + product[2 * rows :]

    head_of = jnp.arange(dlocal, dtype=jnp.int32) // HDIM
    own_head = head_of[None, :] == jnp.arange(local_heads, dtype=jnp.int32)[:, None]
    probe = jnp.where(own_head, pool_query[None, :], 0).astype(bf16)
    probe_keys = dot(probe, pool_kv[0], nt) * (1.0 / math.sqrt(HDIM))
    probe_keys = jnp.concatenate(split_bf16(probe_keys, 2), axis=0).reshape(-1, pmax)
    probe_rows = probe_keys.shape[0]
    padding = jnp.zeros((-probe_rows % 16, pmax), bf16)

    own_x = jnp.concatenate([patches[0].T, patches[1].T, probe_keys, padding], axis=0)
    left_x, right_x = shift(own_x, 1), shift(own_x, -1)

    texts = spread_all(text_emb, "plane").reshape(-1, width)
    texts, left_x, right_x = lax.optimization_barrier((texts, left_x, right_x))
    far_a, far_b = shift(left_x[:dlocal], 1), shift(right_x[dlocal:], -1)
    came = [own_x[2 * dlocal :], right_x[2 * dlocal :], far_b[dlocal:], left_x[2 * dlocal :]]
    came = [x[:probe_rows] for x in came]
    probe_all = jnp.stack([lax.select_n((j - me) % shards, *came) for j in range(shards)])
    probe_all = probe_all.reshape(shards, 2, local_heads, width).transpose(1, 0, 2, 3).reshape(2 * heads, width)

    my_image, my_half = me // 2, me % 2
    w_rows = w_qkv.transpose(0, 2, 1).reshape(3 * dlocal, width)
    gain = ln1_gain[:, None]
    my_count = jnp.where(my_image == 0, patch_count[0], patch_count[1])
    other_count = jnp.where(my_image == 0, patch_count[1], patch_count[0])
    slices = (own_x, left_x, right_x, far_a, far_b)
    first, _ = attend((me, 1 - my_image, other_count), slices, w_rows, w_out, gain)
    second, mine = attend((me, my_image, my_count), slices, w_rows, w_out, gain)

    quarter = half // 2
    even = my_half == 0
    far = jnp.where(even, first[:half], first[half:])
    far_after, far_before = shift(far[:quarter], 1), shift(far[quarter:], -1)
    after = jnp.where(even, second[half:], first[:half])
    before = jnp.where(even, first[half:], second[:half])
    own_part = jnp.where(even, second[:half], second[half:]).astype(f32)

    def added(left, right):
        return (left.astype(f32) + right.astype(f32)).astype(bf16)

    after = jnp.concatenate([added(after[:quarter], far_after), after[quarter:]], axis=0)
    before = jnp.concatenate([before[:quarter], added(before[quarter:], far_before)], axis=0)
    parts = own_part + shift(after, 1).astype(f32) + shift(before, -1).astype(f32)
    resid = jnp.where(my_half == 0, mine[:, :half], mine[:, half:]).T
    stream = (resid.astype(f32) + parts).astype(bf16)
    normed2 = layer_norm(stream, ln2_gain).astype(bf16)
    both = dot(probe_all, normed2, nt)
    pool_scores = both[:heads] + both[heads:]
    row_ids = my_half * half + jnp.arange(half, dtype=jnp.int32)
    pool_scores = jnp.where((row_ids < my_count)[None, :], pool_scores, -1e30)
    highest = jnp.max(pool_scores, axis=-1, keepdims=True)
    raised = jnp.exp(pool_scores - highest)
    total = jnp.sum(raised, axis=-1, keepdims=True)
    mixed = dot((raised / total).astype(bf16), normed2)
    lse = jnp.broadcast_to(highest + jnp.log(total), (heads, 128))
    send = jnp.concatenate([mixed, lse], axis=1).reshape(shards, local_heads, width + 128)
    halves = lax.all_to_all(send, "mp", 0, 0).reshape(shards * local_heads, width + 128)
    shares = pool_embed(halves, pool_kv.transpose(0, 2, 1), pool_out)


    pairs = jnp.broadcast_to(image_pair.astype(f32)[:, None], (rows_img, 128))
    column = spread_all(jnp.concatenate([shares, pairs], axis=1), ("near", "mp"))
    column = column.reshape(-1, shards, rows_img, width + 128)
    embeds = jnp.sum(column[..., :width], axis=1)
    inv_img = lax.rsqrt(jnp.sum(embeds * embeds, axis=-1, keepdims=True) + 1e-06)
    zimg = embeds * inv_img

    scale = jnp.exp(logit_scale)
    planes, nears = texts.shape[0] // rows_img, embeds.shape[0]
    near = lax.axis_index("near")
    z_part = zimg.reshape(-1, width)
    pair_part = column[:, 0, :, width].reshape(-1)
    plane_ids = jnp.arange(planes, dtype=jnp.int32)[:, None] * nears + near
    text_ids = (plane_ids * rows_img + jnp.arange(rows_img, dtype=jnp.int32)[None, :]).reshape(-1)
    texts_f32 = texts.astype(f32)
    inv_txt = lax.rsqrt(jnp.sum(texts_f32 * texts_f32, axis=-1) + 1e-06)
    logits = scale * dot_exact(z_part, texts, nt) * inv_txt[None, :] + logit_bias
    is_pair = pair_part.astype(jnp.int32)[:, None] == text_ids[None, :]
    label = jnp.where(is_pair, 1.0, -1.0).astype(f32)
    dlog = -label * jax.nn.sigmoid(-label * logits) * scale
    gimg = dot_exact(dlog * inv_txt[None, :], texts).reshape(nears, rows_img, width)
    gtxt = jnp.dot(dlog.T, z_part, precision=lax.Precision.HIGHEST).reshape(planes, rows_img, width)

    gtxt = jnp.sum(lax.all_to_all(gtxt, "plane", 0, 0), axis=0)
    gimg_own = lax.dynamic_index_in_dim(gimg, near, 0, False)
    for k in range(1, nears):
        gimg_own += shift(lax.dynamic_index_in_dim(gimg, (near + k) % nears, 0, False), k, "near")
    gimg = gimg_own

    zimg_own = lax.dynamic_index_in_dim(zimg, near, 0, False)
    inv_img_own = lax.dynamic_index_in_dim(inv_img, near, 0, False)
    text_own = text_emb.astype(f32)
    inv_txt_own = lax.rsqrt(jnp.sum(text_own * text_own, axis=-1, keepdims=True) + 1e-06)
    ztxt_own = text_own * inv_txt_own
    image_grad = (gimg - zimg_own * jnp.sum(zimg_own * gimg, axis=-1, keepdims=True)) * inv_img_own
    text_grad = (gtxt - ztxt_own * jnp.sum(ztxt_own * gtxt, axis=-1, keepdims=True)) * inv_txt_own
    return (image_grad, text_grad)


def solution(mesh):
    devices = mesh.devices.reshape(-1, 4, mesh.shape["mp"])
    fine = jax.sharding.Mesh(devices, ("plane", "near", "mp"))
    dp = ("plane", "near")
    placed = (
        P(dp, None, "mp"),
        P(dp),
        P(),
        P(None, None, "mp"),
        P("mp", None),
        P(),
        P(None, None, "mp"),
        P("mp"),
        P("mp", None),
        P(dp, None),
        P(dp),
        P(),
        P(),
    )
    return jax.shard_map(
        per_device,
        mesh=fine,
        in_specs=placed,
        out_specs=(P(dp, None), P(dp, None)),
        check_vma=False,
    )
```

```python
import math

import jax
import jax.numpy as jnp
from jax import lax
from jax.experimental import pallas as pl
from jax.experimental.pallas import tpu as pltpu
from jax.sharding import PartitionSpec as P

HDIM = 72


def spread_all(value, axis):
    count = lax.axis_size(axis)
    return lax.all_to_all(jnp.broadcast_to(value[None], (count,) + value.shape), axis, 0, 0)


def shift(value, steps, axis="mp"):
    count = lax.axis_size(axis)
    pairs = [(source, (source + steps) % count) for source in range(count)]
    return lax.ppermute(value, axis, pairs)


def layer_norm(values, gain_vec):
    floats = values.astype(jnp.float32)
    center = floats - jnp.mean(floats, axis=-1, keepdims=True)
    spread = jnp.mean(center * center, axis=-1, keepdims=True)
    return center * lax.rsqrt(spread + 1e-06) * gain_vec


def split_bf16(values, terms):
    pieces = []
    for _ in range(terms):
        top = values.astype(jnp.bfloat16)
        pieces.append(top)
        values = values - top.astype(jnp.float32)
    return pieces


def matmul(left, right, dims=(((1,), (0,)), ((), ()))):
    return lax.dot_general(left, right, dims, preferred_element_type=jnp.float32)


NT = (((1,), (1,)), ((), ()))


def attend_kernel(scalar_ref, own_ref, left_ref, right_ref, far_a_ref, far_b_ref, w_ref, out_w_ref, gain_ref,
                  o_ref, x_ref, norm_ref, ctx_ref):
    f32, bf16 = jnp.float32, jnp.bfloat16
    width, pmax = x_ref.shape
    dlocal = out_w_ref.shape[0]
    shards = width // dlocal
    me, image, count = scalar_ref[0], scalar_ref[1], scalar_ref[2]
    far = jnp.where(image == 0, far_a_ref[...].astype(f32), far_b_ref[...].astype(f32))
    slices = [ref[...].astype(f32) for ref in (own_ref, left_ref, right_ref)] + [far]
    mean = sum(jnp.sum(part, axis=0, keepdims=True) for part in slices) * (1.0 / width)
    centers = [part - mean for part in slices]
    spread = sum(jnp.sum(part * part, axis=0, keepdims=True) for part in centers) * (1.0 / width)
    scale = lax.rsqrt(spread + 1e-06)
    for part, center, steps in zip(slices, centers, (0, shards - 1, 1, 2)):
        source = lax.rem(me + steps, shards)
        place = pl.ds(pl.multiple_of(source * dlocal, 16), dlocal)
        x_ref[place] = part.astype(bf16)
        norm_ref[place] = (center * scale * gain_ref[place]).astype(bf16)
    proj = matmul(w_ref[...], norm_ref[...])
    live = lax.broadcasted_iota(jnp.int32, (pmax, pmax), 0) < count
    for h in range(dlocal // HDIM):
        q, k, v = (proj[c * dlocal + h * HDIM : c * dlocal + (h + 1) * HDIM] for c in range(3))
        scores = matmul(k.T.astype(bf16), q.astype(bf16)) * (1.0 / math.sqrt(HDIM))
        scores = jnp.where(live, scores, -1e30)
        raised = jnp.exp(scores - jnp.max(scores, axis=0, keepdims=True))
        total = jnp.sum(raised, axis=0, keepdims=True)
        ctx_ref[h * HDIM : (h + 1) * HDIM] = matmul(v.astype(bf16), raised.astype(bf16)) / total
    context = ctx_ref[...].T.astype(bf16)
    o_ref[...] = matmul(context, out_w_ref[...]).astype(bf16)


def attend(scalars, slices, w_rows, w_out, gain):
    pmax = slices[0].shape[1]
    dlocal, width = w_out.shape
    flops = 16 * pmax * (3 * dlocal * width + 2 * dlocal * pmax + dlocal * width)
    of_image = pl.BlockSpec((dlocal, pmax), lambda i, scalar_ref: (scalar_ref[1], 0))
    whole = lambda *shape: pl.BlockSpec(shape, lambda i, scalar_ref: (0, 0))
    return pl.pallas_call(
        attend_kernel,
        grid_spec=pltpu.PrefetchScalarGridSpec(
            num_scalar_prefetch=1,
            grid=(1,),
            in_specs=[of_image] * 3
            + [whole(dlocal, pmax)] * 2
            + [whole(3 * dlocal, width), whole(dlocal, width), whole(width, 1)],
            out_specs=[whole(pmax, width), whole(width, pmax)],
            scratch_shapes=[pltpu.VMEM((width, pmax), jnp.bfloat16), pltpu.VMEM((dlocal, pmax), jnp.float32)],
        ),
        out_shape=[
            jax.ShapeDtypeStruct((pmax, width), jnp.bfloat16),
            jax.ShapeDtypeStruct((width, pmax), jnp.bfloat16),
        ],
        compiler_params=pltpu.CompilerParams(vmem_limit_bytes=32 * 1024 * 1024),
        cost_estimate=pl.CostEstimate(
            flops=flops, bytes_accessed=8 * width * dlocal + 8 * pmax * width, transcendentals=0
        ),
        name="attend",
    )(jnp.stack(scalars).astype(jnp.int32), *slices, w_rows, w_out, gain)


def mix_kernel(scalar_ref, own_ref, after_ref, before_ref, x_ref, gain_ref, probe_ref, o_ref):
    f32, bf16 = jnp.float32, jnp.bfloat16
    half, width = own_ref.shape
    heads = probe_ref.shape[0] // 2
    stream = x_ref[...].astype(f32).T + (
        own_ref[...].astype(f32) + after_ref[:half].astype(f32) + before_ref[...].astype(f32)
    )
    normed = layer_norm(stream.astype(bf16), gain_ref[...]).astype(bf16)
    scores = matmul(probe_ref[...], normed, NT)
    scores = scores[:heads] + scores[heads:]
    row = scalar_ref[0] * half + lax.broadcasted_iota(jnp.int32, (heads, half), 1)
    scores = jnp.where(row < scalar_ref[1], scores, -1e30)
    highest = jnp.max(scores, axis=1, keepdims=True)
    raised = jnp.exp(scores - highest)
    total = jnp.sum(raised, axis=1, keepdims=True)
    o_ref[:, :width] = matmul((raised / total).astype(bf16), normed)
    o_ref[:, width:] = jnp.broadcast_to(highest + jnp.log(total), (heads, o_ref.shape[1] - width))


def mix_rows(my_half, count, second, after, before, mine, gain, probe_all):
    half, width = before.shape
    heads = probe_all.shape[0] // 2
    whole = lambda *shape: pl.BlockSpec(shape, lambda i, scalar_ref: (0, 0))
    return pl.pallas_call(
        mix_kernel,
        grid_spec=pltpu.PrefetchScalarGridSpec(
            num_scalar_prefetch=1,
            grid=(1,),
            in_specs=[
                pl.BlockSpec((half, width), lambda i, scalar_ref: (scalar_ref[0], 0)),
                whole(*after.shape),
                whole(half, width),
                pl.BlockSpec((width, half), lambda i, scalar_ref: (0, scalar_ref[0])),
                whole(1, width),
                whole(2 * heads, width),
            ],
            out_specs=whole(heads, width + 128),
        ),
        out_shape=jax.ShapeDtypeStruct((heads, width + 128), jnp.float32),
        compiler_params=pltpu.CompilerParams(vmem_limit_bytes=16 * 1024 * 1024),
        name="mix_rows",
    )(jnp.stack([my_half, count]).astype(jnp.int32), second, after, before, mine, gain, probe_all)


def pool_kernel(halves_ref, val_ref, out_w_ref, o_ref):
    f32, bf16 = jnp.float32, jnp.bfloat16
    dlocal, width = out_w_ref.shape
    heads = dlocal // HDIM
    images = halves_ref.shape[0] // (2 * heads)
    mixed = []
    for i in range(images):
        first = halves_ref[2 * i * heads : (2 * i + 1) * heads]
        second = halves_ref[(2 * i + 1) * heads : (2 * i + 2) * heads]
        lse_a, lse_b = first[:, width : width + 1], second[:, width : width + 1]
        top = jnp.maximum(lse_a, lse_b)
        raised_a, raised_b = jnp.exp(lse_a - top), jnp.exp(lse_b - top)
        total = raised_a + raised_b
        mixed.append(first[:, :width] * (raised_a / total) + second[:, :width] * (raised_b / total))
    mixed = jnp.concatenate(mixed, axis=0)
    rows = images * heads
    terms = []
    for _ in range(2):
        top = mixed.astype(bf16).astype(f32)
        terms.append(top)
        mixed = mixed - top
    vals = matmul(jnp.concatenate(terms, axis=0).astype(bf16), val_ref[0], NT)
    vals = vals[:rows] + vals[rows:]
    row = lax.broadcasted_iota(jnp.int32, (rows, dlocal), 0)
    lane = lax.broadcasted_iota(jnp.int32, (rows, dlocal), 1)
    start = (row % heads) * HDIM
    vals = jnp.where((lane >= start) & (lane < start + HDIM), vals, 0.0)
    pooled = [jnp.sum(vals[i * heads : (i + 1) * heads], axis=0, keepdims=True) for i in range(images)]
    pooled.append(jnp.zeros((16 - images, dlocal), f32))
    pooled = jnp.concatenate(pooled, axis=0).astype(bf16)
    o_ref[...] = matmul(pooled, out_w_ref[...])[:images]


def pool_embed(halves, pool_kv_rows, pool_out):
    dlocal, width = pool_out.shape
    images = halves.shape[0] // (2 * (dlocal // HDIM))
    return pl.pallas_call(
        pool_kernel,
        grid=(1,),
        in_specs=[
            pl.BlockSpec(halves.shape, lambda i: (0, 0)),
            pl.BlockSpec((1, dlocal, width), lambda i: (1, 0, 0)),
            pl.BlockSpec((dlocal, width), lambda i: (0, 0)),
        ],
        out_specs=pl.BlockSpec((images, width), lambda i: (0, 0)),
        out_shape=jax.ShapeDtypeStruct((images, width), jnp.float32),
        compiler_params=pltpu.CompilerParams(vmem_limit_bytes=12 * 1024 * 1024),
        name="pool_embed",
    )(halves, pool_kv_rows, pool_out)


def per_device(
    patches,
    patch_count,
    ln1_gain,
    w_qkv,
    w_out,
    ln2_gain,
    pool_kv,
    pool_query,
    pool_out,
    text_emb,
    image_pair,
    logit_scale,
    logit_bias,
):
    f32, bf16 = jnp.float32, jnp.bfloat16
    rows_img, pmax, dlocal = patches.shape
    width = w_out.shape[1]
    local_heads = dlocal // HDIM
    heads = width // HDIM
    shards = lax.axis_size("mp")
    me = lax.axis_index("mp")
    half = pmax // 2
    nt = (((1,), (1,)), ((), ()))

    def dot(left, right, dims=(((1,), (0,)), ((), ()))):
        return lax.dot_general(left, right, dims, preferred_element_type=f32)

    def dot_exact(left, right, dims=(((1,), (0,)), ((), ()))):
        rows = left.shape[0]
        product = dot(jnp.concatenate(split_bf16(left, 3), axis=0), right, dims)
        return product[:rows] + product[rows : 2 * rows] + product[2 * rows :]

    head_of = jnp.arange(dlocal, dtype=jnp.int32) // HDIM
    own_head = head_of[None, :] == jnp.arange(local_heads, dtype=jnp.int32)[:, None]
    probe = jnp.where(own_head, pool_query[None, :], 0).astype(bf16)
    probe_keys = dot(probe, pool_kv[0], nt) * (1.0 / math.sqrt(HDIM))
    probe_keys = jnp.concatenate(split_bf16(probe_keys, 2), axis=0)
    probe_rows = probe_keys.shape[0]

    own_x = patches.transpose(0, 2, 1).reshape(rows_img * dlocal, pmax)
    left_x, right_x = shift(own_x, 1), shift(own_x, -1)
    texts = spread_all(text_emb, "plane").reshape(-1, width)
    texts, left_x, right_x = lax.optimization_barrier((texts, left_x, right_x))
    far_a, far_b = shift(left_x[:dlocal], 1), shift(right_x[dlocal:], -1)

    my_image, my_half = me // 2, me % 2
    w_rows = w_qkv.transpose(0, 2, 1).reshape(3 * dlocal, width)
    gain = ln1_gain[:, None]
    my_count = jnp.where(my_image == 0, patch_count[0], patch_count[1])
    other_count = jnp.where(my_image == 0, patch_count[1], patch_count[0])
    slices = (own_x, left_x, right_x, far_a, far_b)
    first, _ = attend((me, 1 - my_image, other_count), slices, w_rows, w_out, gain)
    second, mine = attend((me, my_image, my_count), slices, w_rows, w_out, gain)

    quarter = half // 2
    even = my_half == 0
    far = jnp.where(even, first[:half], first[half:])
    tail = jnp.concatenate([probe_keys, jnp.zeros((-probe_rows % 16, width), bf16)], axis=0)
    far_after = shift(jnp.concatenate([far[:quarter], tail], axis=0), 1)
    far_before = shift(jnp.concatenate([far[quarter:], tail], axis=0), -1)
    left_keys, right_keys = far_after[quarter:], far_before[quarter:]
    far_after, far_before = far_after[:quarter], far_before[:quarter]
    after = jnp.where(even, second[half:], first[:half])
    before = jnp.where(even, first[half:], second[:half])

    def added(left, right):
        return (left.astype(f32) + right.astype(f32)).astype(bf16)

    after = jnp.concatenate([added(after[:quarter], far_after), after[quarter:], left_keys], axis=0)
    before = jnp.concatenate([before[:quarter], added(before[quarter:], far_before)], axis=0)
    after, before = shift(after, 1), shift(before, -1)
    came = [x[:probe_rows] for x in (tail, right_keys, after[half:], left_keys)]
    keys = [lax.select_n((j - me) % shards, *came) for j in range(shards)]
    probe_all = jnp.concatenate([k[:local_heads] for k in keys] + [k[local_heads:] for k in keys], axis=0)
    send = mix_rows(my_half, my_count, second, after, before, mine, ln2_gain[None], probe_all)
    send = send.reshape(shards, local_heads, width + 128)
    halves = lax.all_to_all(send, "mp", 0, 0).reshape(shards * local_heads, width + 128)
    shares = pool_embed(halves, pool_kv.transpose(0, 2, 1), pool_out)


    pairs = jnp.broadcast_to(image_pair.astype(bf16)[:, None], (rows_img, 128))
    column = spread_all(jnp.concatenate([shares.astype(bf16), pairs], axis=1), ("near", "mp"))
    column = column.reshape(-1, shards, rows_img, width + 128).astype(f32)
    embeds = jnp.sum(column[..., :width], axis=1)
    inv_img = lax.rsqrt(jnp.sum(embeds * embeds, axis=-1, keepdims=True) + 1e-06)
    zimg = embeds * inv_img

    scale = jnp.exp(logit_scale)
    planes, nears = texts.shape[0] // rows_img, embeds.shape[0]
    near = lax.axis_index("near")
    z_part = zimg.reshape(-1, width)
    pair_part = column[:, 0, :, width].reshape(-1)
    plane_ids = jnp.arange(planes, dtype=jnp.int32)[:, None] * nears + near
    text_ids = (plane_ids * rows_img + jnp.arange(rows_img, dtype=jnp.int32)[None, :]).reshape(-1)
    texts_f32 = texts.astype(f32)
    inv_txt = lax.rsqrt(jnp.sum(texts_f32 * texts_f32, axis=-1) + 1e-06)
    logits = scale * dot_exact(z_part, texts, nt) * inv_txt[None, :] + logit_bias
    is_pair = pair_part.astype(jnp.int32)[:, None] == text_ids[None, :]
    label = jnp.where(is_pair, 1.0, -1.0).astype(f32)
    dlog = -label * jax.nn.sigmoid(-label * logits) * scale
    gimg = dot_exact(dlog * inv_txt[None, :], texts).reshape(nears, rows_img, width)
    gtxt = jnp.dot(dlog.T, z_part, precision=lax.Precision.HIGHEST).reshape(planes, rows_img, width)

    gtxt = jnp.sum(lax.all_to_all(gtxt.astype(bf16), "plane", 0, 0).astype(f32), axis=0)
    gimg_own = lax.dynamic_index_in_dim(gimg, near, 0, False)
    gimg_own, gtxt = lax.optimization_barrier((gimg_own, gtxt))
    for k in range(1, nears):
        gimg_own += shift(lax.dynamic_index_in_dim(gimg, (near + k) % nears, 0, False), k, "near")
    gimg = gimg_own

    zimg_own = lax.dynamic_index_in_dim(zimg, near, 0, False)
    inv_img_own = lax.dynamic_index_in_dim(inv_img, near, 0, False)
    text_own = text_emb.astype(f32)
    inv_txt_own = lax.rsqrt(jnp.sum(text_own * text_own, axis=-1, keepdims=True) + 1e-06)
    ztxt_own = text_own * inv_txt_own
    image_grad = (gimg - zimg_own * jnp.sum(zimg_own * gimg, axis=-1, keepdims=True)) * inv_img_own
    text_grad = (gtxt - ztxt_own * jnp.sum(ztxt_own * gtxt, axis=-1, keepdims=True)) * inv_txt_own
    return (image_grad, text_grad)


def solution(mesh):
    devices = mesh.devices.reshape(-1, 4, mesh.shape["mp"])
    fine = jax.sharding.Mesh(devices, ("plane", "near", "mp"))
    dp = ("plane", "near")
    placed = (
        P(dp, None, "mp"),
        P(dp),
        P(),
        P(None, None, "mp"),
        P("mp", None),
        P(),
        P(None, None, "mp"),
        P("mp"),
        P("mp", None),
        P(dp, None),
        P(dp),
        P(),
        P(),
    )
    return jax.shard_map(
        per_device,
        mesh=fine,
        in_specs=placed,
        out_specs=(P(dp, None), P(dp, None)),
        check_vma=False,
    )
```

```python
import math

import jax
import jax.numpy as jnp
from jax import lax
from jax.experimental import pallas as pl
from jax.experimental.pallas import tpu as pltpu
from jax.sharding import PartitionSpec as P

HDIM = 72


def spread_all(value, axis):
    count = lax.axis_size(axis)
    return lax.all_to_all(jnp.broadcast_to(value[None], (count,) + value.shape), axis, 0, 0)


def shift(value, steps, axis="mp"):
    count = lax.axis_size(axis)
    pairs = [(source, (source + steps) % count) for source in range(count)]
    return lax.ppermute(value, axis, pairs)


def layer_norm(values, gain_vec):
    floats = values.astype(jnp.float32)
    center = floats - jnp.mean(floats, axis=-1, keepdims=True)
    spread = jnp.mean(center * center, axis=-1, keepdims=True)
    return center * lax.rsqrt(spread + 1e-06) * gain_vec


def split_bf16(values, terms):
    pieces = []
    for _ in range(terms):
        top = values.astype(jnp.bfloat16)
        pieces.append(top)
        values = values - top.astype(jnp.float32)
    return pieces


def matmul(left, right, dims=(((1,), (0,)), ((), ()))):
    return lax.dot_general(left, right, dims, preferred_element_type=jnp.float32)


NT = (((1,), (1,)), ((), ()))


def attend_kernel(scalar_ref, own_ref, left_ref, right_ref, far_a_ref, far_b_ref, w_ref, out_w_ref, gain_ref,
                  o_ref, base_ref, x_ref, norm_ref, ctx_ref):
    f32, bf16 = jnp.float32, jnp.bfloat16
    width, pmax = x_ref.shape
    dlocal = out_w_ref.shape[0]
    shards = width // dlocal
    me, image, count = scalar_ref[0], scalar_ref[1], scalar_ref[2]
    far = jnp.where(image == 0, far_a_ref[...].astype(f32), far_b_ref[...].astype(f32))
    slices = [ref[...].astype(f32) for ref in (own_ref, left_ref, right_ref)] + [far]
    mean = sum(jnp.sum(part, axis=0, keepdims=True) for part in slices) * (1.0 / width)
    centers = [part - mean for part in slices]
    spread = sum(jnp.sum(part * part, axis=0, keepdims=True) for part in centers) * (1.0 / width)
    scale = lax.rsqrt(spread + 1e-06)
    for part, center, steps in zip(slices, centers, (0, shards - 1, 1, 2)):
        source = lax.rem(me + steps, shards)
        place = pl.ds(pl.multiple_of(source * dlocal, 16), dlocal)
        x_ref[place] = part.astype(bf16)
        norm_ref[place] = (center * scale * gain_ref[place]).astype(bf16)
    proj = matmul(w_ref[...], norm_ref[...])
    live = lax.broadcasted_iota(jnp.int32, (pmax, pmax), 0) < count
    for h in range(dlocal // HDIM):
        q, k, v = (proj[c * dlocal + h * HDIM : c * dlocal + (h + 1) * HDIM] for c in range(3))
        scores = matmul(k.T.astype(bf16), q.astype(bf16)) * (1.0 / math.sqrt(HDIM))
        scores = jnp.where(live, scores, -1e30)
        raised = jnp.exp(scores - jnp.max(scores, axis=0, keepdims=True))
        total = jnp.sum(raised, axis=0, keepdims=True)
        ctx_ref[h * HDIM : (h + 1) * HDIM] = matmul(v.astype(bf16), raised.astype(bf16)) / total
    context = ctx_ref[...].T.astype(bf16)
    out = matmul(context, out_w_ref[...])
    o_ref[...] = out.astype(bf16)
    half = pmax // 2
    first_half = scalar_ref[3] == 0
    resid = jnp.where(first_half, x_ref[:, :half].astype(f32), x_ref[:, half:].astype(f32))
    base_ref[...] = resid.T + jnp.where(first_half, out[:half], out[half:])


def attend(scalars, slices, w_rows, w_out, gain):
    pmax = slices[0].shape[1]
    dlocal, width = w_out.shape
    flops = 16 * pmax * (3 * dlocal * width + 2 * dlocal * pmax + dlocal * width)
    of_image = pl.BlockSpec((dlocal, pmax), lambda i, scalar_ref: (scalar_ref[1], 0))
    whole = lambda *shape: pl.BlockSpec(shape, lambda i, scalar_ref: (0, 0))
    return pl.pallas_call(
        attend_kernel,
        grid_spec=pltpu.PrefetchScalarGridSpec(
            num_scalar_prefetch=1,
            grid=(1,),
            in_specs=[of_image] * 3
            + [whole(dlocal, pmax)] * 2
            + [whole(3 * dlocal, width), whole(dlocal, width), whole(width, 1)],
            out_specs=[whole(pmax, width), whole(pmax // 2, width)],
            scratch_shapes=[
                pltpu.VMEM((width, pmax), jnp.bfloat16),
                pltpu.VMEM((width, pmax), jnp.bfloat16),
                pltpu.VMEM((dlocal, pmax), jnp.float32),
            ],
        ),
        out_shape=[
            jax.ShapeDtypeStruct((pmax, width), jnp.bfloat16),
            jax.ShapeDtypeStruct((pmax // 2, width), jnp.float32),
        ],
        compiler_params=pltpu.CompilerParams(vmem_limit_bytes=32 * 1024 * 1024),
        cost_estimate=pl.CostEstimate(
            flops=flops, bytes_accessed=8 * width * dlocal + 8 * pmax * width, transcendentals=0
        ),
        name="attend",
    )(jnp.stack(scalars).astype(jnp.int32), *slices, w_rows, w_out, gain)


def mix_kernel(scalar_ref, base_ref, after_ref, before_ref, gain_ref, own_ref, right_ref, left_ref, o_ref):
    f32, bf16 = jnp.float32, jnp.bfloat16
    half, width = base_ref.shape
    shards, local = o_ref.shape[:2]
    heads, block = shards * local, own_ref.shape[0]
    stream = base_ref[...] + after_ref[:half].astype(f32) + before_ref[...].astype(f32)
    normed = layer_norm(stream.astype(bf16), gain_ref[...]).astype(bf16)
    keys = jnp.concatenate([own_ref[...], right_ref[...], after_ref[half:], left_ref[...]], axis=0)
    both = matmul(keys, normed, NT)
    scores = jnp.concatenate(
        [both[k * block : k * block + local] + both[k * block + local : k * block + 2 * local] for k in range(shards)],
        axis=0,
    )
    row = scalar_ref[0] * half + lax.broadcasted_iota(jnp.int32, (heads, half), 1)
    scores = jnp.where(row < scalar_ref[1], scores, -1e30)
    highest = jnp.max(scores, axis=1, keepdims=True)
    raised = jnp.exp(scores - highest)
    total = jnp.sum(raised, axis=1, keepdims=True)
    mixed = matmul((raised / total).astype(bf16), normed)
    lse = jnp.broadcast_to(highest + jnp.log(total), (heads, o_ref.shape[2] - width))
    for k in range(shards):
        source = lax.rem(scalar_ref[2] + k, shards)
        o_ref[source, :, :width] = mixed[k * local : (k + 1) * local]
        o_ref[source, :, width:] = lse[k * local : (k + 1) * local]


def mix_rows(scalars, base, after, before, gain, own_keys, right_keys, left_keys, shards, local):
    half, width = before.shape
    whole = lambda *shape: pl.BlockSpec(shape, lambda i, scalar_ref: (0,) * len(shape))
    operands = (base, after, before, gain, own_keys, right_keys, left_keys)
    return pl.pallas_call(
        mix_kernel,
        grid_spec=pltpu.PrefetchScalarGridSpec(
            num_scalar_prefetch=1,
            grid=(1,),
            in_specs=[whole(*x.shape) for x in operands],
            out_specs=whole(shards, local, width + 128),
        ),
        out_shape=jax.ShapeDtypeStruct((shards, local, width + 128), jnp.float32),
        compiler_params=pltpu.CompilerParams(vmem_limit_bytes=16 * 1024 * 1024),
        name="mix_rows",
    )(jnp.stack(scalars).astype(jnp.int32), *operands)


def pool_kernel(halves_ref, val_ref, out_w_ref, o_ref):
    f32, bf16 = jnp.float32, jnp.bfloat16
    dlocal, width = out_w_ref.shape
    heads = dlocal // HDIM
    images = halves_ref.shape[0] // (2 * heads)
    mixed = []
    for i in range(images):
        first = halves_ref[2 * i * heads : (2 * i + 1) * heads]
        second = halves_ref[(2 * i + 1) * heads : (2 * i + 2) * heads]
        lse_a, lse_b = first[:, width : width + 1], second[:, width : width + 1]
        top = jnp.maximum(lse_a, lse_b)
        raised_a, raised_b = jnp.exp(lse_a - top), jnp.exp(lse_b - top)
        total = raised_a + raised_b
        mixed.append(first[:, :width] * (raised_a / total) + second[:, :width] * (raised_b / total))
    mixed = jnp.concatenate(mixed, axis=0)
    rows = images * heads
    terms = []
    for _ in range(2):
        top = mixed.astype(bf16).astype(f32)
        terms.append(top)
        mixed = mixed - top
    vals = matmul(jnp.concatenate(terms, axis=0).astype(bf16), val_ref[0], NT)
    vals = vals[:rows] + vals[rows:]
    row = lax.broadcasted_iota(jnp.int32, (rows, dlocal), 0)
    lane = lax.broadcasted_iota(jnp.int32, (rows, dlocal), 1)
    start = (row % heads) * HDIM
    vals = jnp.where((lane >= start) & (lane < start + HDIM), vals, 0.0)
    pooled = [jnp.sum(vals[i * heads : (i + 1) * heads], axis=0, keepdims=True) for i in range(images)]
    pooled.append(jnp.zeros((16 - images, dlocal), f32))
    pooled = jnp.concatenate(pooled, axis=0).astype(bf16)
    o_ref[...] = matmul(pooled, out_w_ref[...])[:images]


def pool_embed(halves, pool_kv_rows, pool_out):
    dlocal, width = pool_out.shape
    images = halves.shape[0] // (2 * (dlocal // HDIM))
    return pl.pallas_call(
        pool_kernel,
        grid=(1,),
        in_specs=[
            pl.BlockSpec(halves.shape, lambda i: (0, 0)),
            pl.BlockSpec((1, dlocal, width), lambda i: (1, 0, 0)),
            pl.BlockSpec((dlocal, width), lambda i: (0, 0)),
        ],
        out_specs=pl.BlockSpec((images, width), lambda i: (0, 0)),
        out_shape=jax.ShapeDtypeStruct((images, width), jnp.float32),
        compiler_params=pltpu.CompilerParams(vmem_limit_bytes=12 * 1024 * 1024),
        name="pool_embed",
    )(halves, pool_kv_rows, pool_out)


def per_device(
    patches,
    patch_count,
    ln1_gain,
    w_qkv,
    w_out,
    ln2_gain,
    pool_kv,
    pool_query,
    pool_out,
    text_emb,
    image_pair,
    logit_scale,
    logit_bias,
):
    f32, bf16 = jnp.float32, jnp.bfloat16
    rows_img, pmax, dlocal = patches.shape
    width = w_out.shape[1]
    local_heads = dlocal // HDIM
    heads = width // HDIM
    shards = lax.axis_size("mp")
    me = lax.axis_index("mp")
    half = pmax // 2
    nt = (((1,), (1,)), ((), ()))

    def dot(left, right, dims=(((1,), (0,)), ((), ()))):
        return lax.dot_general(left, right, dims, preferred_element_type=f32)

    def dot_exact(left, right, dims=(((1,), (0,)), ((), ()))):
        rows = left.shape[0]
        product = dot(jnp.concatenate(split_bf16(left, 3), axis=0), right, dims)
        return product[:rows] + product[rows : 2 * rows] + product[2 * rows :]

    head_of = jnp.arange(dlocal, dtype=jnp.int32) // HDIM
    own_head = head_of[None, :] == jnp.arange(local_heads, dtype=jnp.int32)[:, None]
    probe = jnp.where(own_head, pool_query[None, :], 0).astype(bf16)
    probe_keys = dot(probe, pool_kv[0], nt) * (1.0 / math.sqrt(HDIM))
    probe_keys = jnp.concatenate(split_bf16(probe_keys, 2), axis=0)
    probe_rows = probe_keys.shape[0]

    own_x = patches.transpose(0, 2, 1).reshape(rows_img * dlocal, pmax)
    left_x, right_x = shift(own_x, 1), shift(own_x, -1)
    texts = spread_all(text_emb, "plane").reshape(-1, width)
    far_a, far_b = shift(left_x[:dlocal], 1), shift(right_x[dlocal:], -1)
    texts, far_a, far_b = lax.optimization_barrier((texts, far_a, far_b))

    my_image, my_half = me // 2, me % 2
    w_rows = w_qkv.transpose(0, 2, 1).reshape(3 * dlocal, width)
    gain = ln1_gain[:, None]
    my_count = jnp.where(my_image == 0, patch_count[0], patch_count[1])
    other_count = jnp.where(my_image == 0, patch_count[1], patch_count[0])
    slices = (own_x, left_x, right_x, far_a, far_b)
    first, _ = attend((me, 1 - my_image, other_count, my_half), slices, w_rows, w_out, gain)
    quarter = half // 2
    even = my_half == 0
    far = jnp.where(even, first[:half], first[half:])
    tail = jnp.concatenate([probe_keys, jnp.zeros((-probe_rows % 16, width), bf16)], axis=0)
    far_after = shift(jnp.concatenate([far[:quarter], tail], axis=0), 1)
    far_before = shift(jnp.concatenate([far[quarter:], tail], axis=0), -1)
    my_count, far_after = lax.optimization_barrier((my_count, far_after))
    second, base = attend((me, my_image, my_count, my_half), slices, w_rows, w_out, gain)
    left_keys, right_keys = far_after[quarter:], far_before[quarter:]
    far_after, far_before = far_after[:quarter], far_before[:quarter]
    after = jnp.where(even, second[half:], first[:half])
    before = jnp.where(even, first[half:], second[:half])

    def added(left, right):
        return (left.astype(f32) + right.astype(f32)).astype(bf16)

    after = jnp.concatenate([added(after[:quarter], far_after), after[quarter:], left_keys], axis=0)
    before = jnp.concatenate([before[:quarter], added(before[quarter:], far_before)], axis=0)
    after, before = shift(after, 1), shift(before, -1)
    send = mix_rows(
        (my_half, my_count, me), base, after, before, ln2_gain[None], tail, right_keys, left_keys, shards, local_heads
    )
    halves = lax.all_to_all(send, "mp", 0, 0).reshape(shards * local_heads, width + 128)
    shares = pool_embed(halves, pool_kv.transpose(0, 2, 1), pool_out)

    pairs = jnp.broadcast_to(image_pair.astype(bf16)[:, None], (rows_img, 128))
    column = spread_all(jnp.concatenate([shares.astype(bf16), pairs], axis=1), ("near", "mp"))
    column = column.reshape(-1, shards, rows_img, width + 128).astype(f32)
    embeds = jnp.sum(column[..., :width], axis=1)
    inv_img = lax.rsqrt(jnp.sum(embeds * embeds, axis=-1, keepdims=True) + 1e-06)
    zimg = embeds * inv_img

    scale = jnp.exp(logit_scale)
    planes, nears = texts.shape[0] // rows_img, embeds.shape[0]
    near = lax.axis_index("near")
    z_part = zimg.reshape(-1, width)
    pair_part = column[:, 0, :, width].reshape(-1)
    plane_ids = jnp.arange(planes, dtype=jnp.int32)[:, None] * nears + near
    text_ids = (plane_ids * rows_img + jnp.arange(rows_img, dtype=jnp.int32)[None, :]).reshape(-1)
    texts_f32 = texts.astype(f32)
    inv_txt = lax.rsqrt(jnp.sum(texts_f32 * texts_f32, axis=-1) + 1e-06)
    logits = scale * dot_exact(z_part, texts, nt) * inv_txt[None, :] + logit_bias
    is_pair = pair_part.astype(jnp.int32)[:, None] == text_ids[None, :]
    label = jnp.where(is_pair, 1.0, -1.0).astype(f32)
    dlog = -label * jax.nn.sigmoid(-label * logits) * scale
    gimg = dot_exact(dlog * inv_txt[None, :], texts).reshape(nears, rows_img, width)
    gtxt = jnp.dot(dlog.T, z_part, precision=lax.Precision.HIGHEST).reshape(planes, rows_img, width)

    gtxt = jnp.sum(lax.all_to_all(gtxt.astype(bf16), "plane", 0, 0).astype(f32), axis=0)
    gimg_own = lax.dynamic_index_in_dim(gimg, near, 0, False)
    gimg_own, gtxt = lax.optimization_barrier((gimg_own, gtxt))
    for k in range(1, nears):
        gimg_own += shift(lax.dynamic_index_in_dim(gimg, (near + k) % nears, 0, False), k, "near")
    gimg = gimg_own

    zimg_own = lax.dynamic_index_in_dim(zimg, near, 0, False)
    inv_img_own = lax.dynamic_index_in_dim(inv_img, near, 0, False)
    text_own = text_emb.astype(f32)
    inv_txt_own = lax.rsqrt(jnp.sum(text_own * text_own, axis=-1, keepdims=True) + 1e-06)
    ztxt_own = text_own * inv_txt_own
    image_grad = (gimg - zimg_own * jnp.sum(zimg_own * gimg, axis=-1, keepdims=True)) * inv_img_own
    text_grad = (gtxt - ztxt_own * jnp.sum(ztxt_own * gtxt, axis=-1, keepdims=True)) * inv_txt_own
    return (image_grad, text_grad)


def solution(mesh):
    devices = mesh.devices.reshape(-1, 4, mesh.shape["mp"])
    fine = jax.sharding.Mesh(devices, ("plane", "near", "mp"))
    dp = ("plane", "near")
    placed = (
        P(dp, None, "mp"),
        P(dp),
        P(),
        P(None, None, "mp"),
        P("mp", None),
        P(),
        P(None, None, "mp"),
        P("mp"),
        P("mp", None),
        P(dp, None),
        P(dp),
        P(),
        P(),
    )
    return jax.shard_map(
        per_device,
        mesh=fine,
        in_specs=placed,
        out_specs=(P(dp, None), P(dp, None)),
        check_vma=False,
    )
```

```python
import math

import jax
import jax.numpy as jnp
from jax import lax
from jax.experimental import pallas as pl
from jax.experimental.pallas import tpu as pltpu
from jax.sharding import PartitionSpec as P

HDIM = 72


def spread_all(value, axis):
    count = lax.axis_size(axis)
    return lax.all_to_all(jnp.broadcast_to(value[None], (count,) + value.shape), axis, 0, 0)


def shift(value, steps, axis="mp"):
    count = lax.axis_size(axis)
    pairs = [(source, (source + steps) % count) for source in range(count)]
    return lax.ppermute(value, axis, pairs)


def layer_norm(values, gain_vec):
    floats = values.astype(jnp.float32)
    center = floats - jnp.mean(floats, axis=-1, keepdims=True)
    spread = jnp.mean(center * center, axis=-1, keepdims=True)
    return center * lax.rsqrt(spread + 1e-06) * gain_vec


def split_bf16(values, terms):
    pieces = []
    for _ in range(terms):
        top = values.astype(jnp.bfloat16)
        pieces.append(top)
        values = values - top.astype(jnp.float32)
    return pieces


def matmul(left, right, dims=(((1,), (0,)), ((), ()))):
    return lax.dot_general(left, right, dims, preferred_element_type=jnp.float32)


NT = (((1,), (1,)), ((), ()))


def attend_kernel(scalar_ref, own_ref, left_ref, right_ref, far_ref, w_ref, out_w_ref, gain_ref,
                  o_ref, base_ref, x_ref, norm_ref, ctx_ref):
    f32, bf16 = jnp.float32, jnp.bfloat16
    width, pmax = x_ref.shape
    dlocal = out_w_ref.shape[0]
    shards = width // dlocal
    me, count = scalar_ref[0], scalar_ref[2]
    slices = [ref[...].astype(f32) for ref in (own_ref, left_ref, right_ref, far_ref)]
    mean = sum(jnp.sum(part, axis=0, keepdims=True) for part in slices) * (1.0 / width)
    centers = [part - mean for part in slices]
    spread = sum(jnp.sum(part * part, axis=0, keepdims=True) for part in centers) * (1.0 / width)
    scale = lax.rsqrt(spread + 1e-06)
    for part, center, steps in zip(slices, centers, (0, shards - 1, 1, 2)):
        source = lax.rem(me + steps, shards)
        place = pl.ds(pl.multiple_of(source * dlocal, 16), dlocal)
        x_ref[place] = part.astype(bf16)
        norm_ref[place] = (center * scale * gain_ref[place]).astype(bf16)
    proj = matmul(w_ref[...], norm_ref[...])
    live = lax.broadcasted_iota(jnp.int32, (pmax, pmax), 0) < count
    for h in range(dlocal // HDIM):
        q, k, v = (proj[c * dlocal + h * HDIM : c * dlocal + (h + 1) * HDIM] for c in range(3))
        scores = matmul(k.T.astype(bf16), q.astype(bf16)) * (1.0 / math.sqrt(HDIM))
        scores = jnp.where(live, scores, -1e30)
        raised = jnp.exp(scores - jnp.max(scores, axis=0, keepdims=True))
        total = jnp.sum(raised, axis=0, keepdims=True)
        ctx_ref[h * HDIM : (h + 1) * HDIM] = matmul(v.astype(bf16), raised.astype(bf16)) / total
    context = ctx_ref[...].T.astype(bf16)
    out = matmul(context, out_w_ref[...])
    o_ref[...] = out.astype(bf16)
    half = pmax // 2
    first_half = scalar_ref[3] == 0
    resid = jnp.where(first_half, x_ref[:, :half].astype(f32), x_ref[:, half:].astype(f32))
    base_ref[...] = resid.T + jnp.where(first_half, out[:half], out[half:])


def attend(scalars, slices, w_rows, w_out, gain):
    pmax = slices[0].shape[1]
    dlocal, width = w_out.shape
    flops = 16 * pmax * (3 * dlocal * width + 2 * dlocal * pmax + dlocal * width)
    of_image = pl.BlockSpec((dlocal, pmax), lambda i, scalar_ref: (scalar_ref[1], 0))
    whole = lambda *shape: pl.BlockSpec(shape, lambda i, scalar_ref: (0, 0))
    return pl.pallas_call(
        attend_kernel,
        grid_spec=pltpu.PrefetchScalarGridSpec(
            num_scalar_prefetch=1,
            grid=(1,),
            in_specs=[of_image] * 3
            + [whole(dlocal, pmax)]
            + [whole(3 * dlocal, width), whole(dlocal, width), whole(width, 1)],
            out_specs=[whole(pmax, width), whole(pmax // 2, width)],
            scratch_shapes=[
                pltpu.VMEM((width, pmax), jnp.bfloat16),
                pltpu.VMEM((width, pmax), jnp.bfloat16),
                pltpu.VMEM((dlocal, pmax), jnp.float32),
            ],
        ),
        out_shape=[
            jax.ShapeDtypeStruct((pmax, width), jnp.bfloat16),
            jax.ShapeDtypeStruct((pmax // 2, width), jnp.float32),
        ],
        compiler_params=pltpu.CompilerParams(vmem_limit_bytes=32 * 1024 * 1024),
        cost_estimate=pl.CostEstimate(
            flops=flops, bytes_accessed=8 * width * dlocal + 8 * pmax * width, transcendentals=0
        ),
        name="attend",
    )(jnp.stack(scalars).astype(jnp.int32), *slices, w_rows, w_out, gain)


def mix_kernel(scalar_ref, base_ref, after_ref, before_ref, gain_ref, own_ref, right_ref, left_ref, o_ref):
    f32, bf16 = jnp.float32, jnp.bfloat16
    half, width = base_ref.shape
    shards, local = o_ref.shape[:2]
    heads, block = shards * local, own_ref.shape[0]
    stream = base_ref[...] + after_ref[:half].astype(f32) + before_ref[...].astype(f32)
    normed = layer_norm(stream.astype(bf16), gain_ref[...]).astype(bf16)
    keys = jnp.concatenate([own_ref[...], right_ref[...], after_ref[half:], left_ref[...]], axis=0)
    both = matmul(keys, normed, NT)
    scores = jnp.concatenate(
        [both[k * block : k * block + local] + both[k * block + local : k * block + 2 * local] for k in range(shards)],
        axis=0,
    )
    row = scalar_ref[0] * half + lax.broadcasted_iota(jnp.int32, (heads, half), 1)
    scores = jnp.where(row < scalar_ref[1], scores, -1e30)
    highest = jnp.max(scores, axis=1, keepdims=True)
    raised = jnp.exp(scores - highest)
    total = jnp.sum(raised, axis=1, keepdims=True)
    mixed = matmul((raised / total).astype(bf16), normed)
    lse = jnp.broadcast_to(highest + jnp.log(total), (heads, o_ref.shape[2] - width))
    for k in range(shards):
        source = lax.rem(scalar_ref[2] + k, shards)
        o_ref[source, :, :width] = mixed[k * local : (k + 1) * local]
        o_ref[source, :, width:] = lse[k * local : (k + 1) * local]


def mix_rows(scalars, base, after, before, gain, own_keys, right_keys, left_keys, shards, local):
    half, width = before.shape
    whole = lambda *shape: pl.BlockSpec(shape, lambda i, scalar_ref: (0,) * len(shape))
    operands = (base, after, before, gain, own_keys, right_keys, left_keys)
    return pl.pallas_call(
        mix_kernel,
        grid_spec=pltpu.PrefetchScalarGridSpec(
            num_scalar_prefetch=1,
            grid=(1,),
            in_specs=[whole(*x.shape) for x in operands],
            out_specs=whole(shards, local, width + 128),
        ),
        out_shape=jax.ShapeDtypeStruct((shards, local, width + 128), jnp.float32),
        compiler_params=pltpu.CompilerParams(vmem_limit_bytes=16 * 1024 * 1024),
        name="mix_rows",
    )(jnp.stack(scalars).astype(jnp.int32), *operands)


def pool_kernel(halves_ref, val_ref, out_w_ref, o_ref):
    f32, bf16 = jnp.float32, jnp.bfloat16
    dlocal, width = out_w_ref.shape
    heads = dlocal // HDIM
    images = halves_ref.shape[0] // (2 * heads)
    mixed = []
    for i in range(images):
        first = halves_ref[2 * i * heads : (2 * i + 1) * heads]
        second = halves_ref[(2 * i + 1) * heads : (2 * i + 2) * heads]
        lse_a, lse_b = first[:, width : width + 1], second[:, width : width + 1]
        top = jnp.maximum(lse_a, lse_b)
        raised_a, raised_b = jnp.exp(lse_a - top), jnp.exp(lse_b - top)
        total = raised_a + raised_b
        mixed.append(first[:, :width] * (raised_a / total) + second[:, :width] * (raised_b / total))
    mixed = jnp.concatenate(mixed, axis=0)
    rows = images * heads
    terms = []
    for _ in range(2):
        top = mixed.astype(bf16).astype(f32)
        terms.append(top)
        mixed = mixed - top
    vals = matmul(jnp.concatenate(terms, axis=0).astype(bf16), val_ref[0], NT)
    vals = vals[:rows] + vals[rows:]
    row = lax.broadcasted_iota(jnp.int32, (rows, dlocal), 0)
    lane = lax.broadcasted_iota(jnp.int32, (rows, dlocal), 1)
    start = (row % heads) * HDIM
    vals = jnp.where((lane >= start) & (lane < start + HDIM), vals, 0.0)
    pooled = [jnp.sum(vals[i * heads : (i + 1) * heads], axis=0, keepdims=True) for i in range(images)]
    pooled.append(jnp.zeros((16 - images, dlocal), f32))
    pooled = jnp.concatenate(pooled, axis=0).astype(bf16)
    o_ref[...] = matmul(pooled, out_w_ref[...])[:images]


def pool_embed(halves, pool_kv_rows, pool_out):
    dlocal, width = pool_out.shape
    images = halves.shape[0] // (2 * (dlocal // HDIM))
    return pl.pallas_call(
        pool_kernel,
        grid=(1,),
        in_specs=[
            pl.BlockSpec(halves.shape, lambda i: (0, 0)),
            pl.BlockSpec((1, dlocal, width), lambda i: (1, 0, 0)),
            pl.BlockSpec((dlocal, width), lambda i: (0, 0)),
        ],
        out_specs=pl.BlockSpec((images, width), lambda i: (0, 0)),
        out_shape=jax.ShapeDtypeStruct((images, width), jnp.float32),
        compiler_params=pltpu.CompilerParams(vmem_limit_bytes=12 * 1024 * 1024),
        name="pool_embed",
    )(halves, pool_kv_rows, pool_out)


def per_device(
    patches,
    patch_count,
    ln1_gain,
    w_qkv,
    w_out,
    ln2_gain,
    pool_kv,
    pool_query,
    pool_out,
    text_emb,
    image_pair,
    logit_scale,
    logit_bias,
):
    f32, bf16 = jnp.float32, jnp.bfloat16
    rows_img, pmax, dlocal = patches.shape
    width = w_out.shape[1]
    local_heads = dlocal // HDIM
    heads = width // HDIM
    shards = lax.axis_size("mp")
    me = lax.axis_index("mp")
    half = pmax // 2
    nt = (((1,), (1,)), ((), ()))

    def dot(left, right, dims=(((1,), (0,)), ((), ()))):
        return lax.dot_general(left, right, dims, preferred_element_type=f32)

    def dot_exact(left, right, dims=(((1,), (0,)), ((), ()))):
        rows = left.shape[0]
        product = dot(jnp.concatenate(split_bf16(left, 3), axis=0), right, dims)
        return product[:rows] + product[rows : 2 * rows] + product[2 * rows :]

    head_of = jnp.arange(dlocal, dtype=jnp.int32) // HDIM
    own_head = head_of[None, :] == jnp.arange(local_heads, dtype=jnp.int32)[:, None]
    probe = jnp.where(own_head, pool_query[None, :], 0).astype(bf16)
    probe_keys = dot(probe, pool_kv[0], nt) * (1.0 / math.sqrt(HDIM))
    probe_keys = jnp.concatenate(split_bf16(probe_keys, 2), axis=0)
    probe_rows = probe_keys.shape[0]

    own_x = patches.transpose(0, 2, 1).reshape(rows_img * dlocal, pmax)
    left_x, right_x = shift(own_x, 1), shift(own_x, -1)
    texts = spread_all(text_emb, "plane").reshape(-1, width)
    next_first, before_last = 1 - ((me + 1) % shards) // 2, ((me - 1) % shards) // 2
    far_first = shift(lax.dynamic_slice(left_x, (next_first * dlocal, 0), (dlocal, pmax)), 1)
    far_last = shift(lax.dynamic_slice(right_x, (before_last * dlocal, 0), (dlocal, pmax)), -1)
    texts, far_last = lax.optimization_barrier((texts, far_last))

    my_image, my_half = me // 2, me % 2
    w_rows = w_qkv.transpose(0, 2, 1).reshape(3 * dlocal, width)
    gain = ln1_gain[:, None]
    my_count = jnp.where(my_image == 0, patch_count[0], patch_count[1])
    other_count = jnp.where(my_image == 0, patch_count[1], patch_count[0])
    slices = (own_x, left_x, right_x)
    first, _ = attend((me, 1 - my_image, other_count, my_half), slices + (far_first,), w_rows, w_out, gain)
    quarter = half // 2
    even = my_half == 0
    far = jnp.where(even, first[:half], first[half:])
    tail = jnp.concatenate([probe_keys, jnp.zeros((-probe_rows % 16, width), bf16)], axis=0)
    far_after = shift(jnp.concatenate([far[:quarter], tail], axis=0), 1)
    far_before = shift(jnp.concatenate([far[quarter:], tail], axis=0), -1)
    my_count, far_after = lax.optimization_barrier((my_count, far_after))
    second, base = attend((me, my_image, my_count, my_half), slices + (far_last,), w_rows, w_out, gain)
    left_keys, right_keys = far_after[quarter:], far_before[quarter:]
    far_after, far_before = far_after[:quarter], far_before[:quarter]
    after = jnp.where(even, second[half:], first[:half])
    before = jnp.where(even, first[half:], second[:half])

    def added(left, right):
        return (left.astype(f32) + right.astype(f32)).astype(bf16)

    after = jnp.concatenate([added(after[:quarter], far_after), after[quarter:], left_keys], axis=0)
    before = jnp.concatenate([before[:quarter], added(before[quarter:], far_before)], axis=0)
    after, before = shift(after, 1), shift(before, -1)
    send = mix_rows(
        (my_half, my_count, me), base, after, before, ln2_gain[None], tail, right_keys, left_keys, shards, local_heads
    )
    halves = lax.all_to_all(send, "mp", 0, 0).reshape(shards * local_heads, width + 128)
    shares = pool_embed(halves, pool_kv.transpose(0, 2, 1), pool_out)

    pairs = jnp.broadcast_to(image_pair.astype(bf16)[:, None], (rows_img, 128))
    column = spread_all(jnp.concatenate([shares.astype(bf16), pairs], axis=1), ("near", "mp"))
    column = column.reshape(-1, shards, rows_img, width + 128).astype(f32)
    embeds = jnp.sum(column[..., :width], axis=1)
    inv_img = lax.rsqrt(jnp.sum(embeds * embeds, axis=-1, keepdims=True) + 1e-06)
    zimg = embeds * inv_img

    scale = jnp.exp(logit_scale)
    planes, nears = texts.shape[0] // rows_img, embeds.shape[0]
    near = lax.axis_index("near")
    z_part = zimg.reshape(-1, width)
    pair_part = column[:, 0, :, width].reshape(-1)
    plane_ids = jnp.arange(planes, dtype=jnp.int32)[:, None] * nears + near
    text_ids = (plane_ids * rows_img + jnp.arange(rows_img, dtype=jnp.int32)[None, :]).reshape(-1)
    texts_f32 = texts.astype(f32)
    inv_txt = lax.rsqrt(jnp.sum(texts_f32 * texts_f32, axis=-1) + 1e-06)
    logits = scale * dot_exact(z_part, texts, nt) * inv_txt[None, :] + logit_bias
    is_pair = pair_part.astype(jnp.int32)[:, None] == text_ids[None, :]
    label = jnp.where(is_pair, 1.0, -1.0).astype(f32)
    dlog = -label * jax.nn.sigmoid(-label * logits) * scale
    gimg = dot_exact(dlog * inv_txt[None, :], texts).reshape(nears, rows_img, width)
    gtxt = jnp.dot(dlog.T, z_part, precision=lax.Precision.HIGHEST).reshape(planes, rows_img, width)

    gtxt = jnp.sum(lax.all_to_all(gtxt.astype(bf16), "plane", 0, 0).astype(f32), axis=0)
    gimg_own = lax.dynamic_index_in_dim(gimg, near, 0, False)
    gimg_own, gtxt = lax.optimization_barrier((gimg_own, gtxt))
    for k in range(1, nears):
        gimg_own += shift(lax.dynamic_index_in_dim(gimg, (near + k) % nears, 0, False), k, "near")
    gimg = gimg_own

    zimg_own = lax.dynamic_index_in_dim(zimg, near, 0, False)
    inv_img_own = lax.dynamic_index_in_dim(inv_img, near, 0, False)
    text_own = text_emb.astype(f32)
    inv_txt_own = lax.rsqrt(jnp.sum(text_own * text_own, axis=-1, keepdims=True) + 1e-06)
    ztxt_own = text_own * inv_txt_own
    image_grad = (gimg - zimg_own * jnp.sum(zimg_own * gimg, axis=-1, keepdims=True)) * inv_img_own
    text_grad = (gtxt - ztxt_own * jnp.sum(ztxt_own * gtxt, axis=-1, keepdims=True)) * inv_txt_own
    return (image_grad, text_grad)


def solution(mesh):
    devices = mesh.devices.reshape(-1, 4, mesh.shape["mp"])
    fine = jax.sharding.Mesh(devices, ("plane", "near", "mp"))
    dp = ("plane", "near")
    placed = (
        P(dp, None, "mp"),
        P(dp),
        P(),
        P(None, None, "mp"),
        P("mp", None),
        P(),
        P(None, None, "mp"),
        P("mp"),
        P("mp", None),
        P(dp, None),
        P(dp),
        P(),
        P(),
    )
    return jax.shard_map(
        per_device,
        mesh=fine,
        in_specs=placed,
        out_specs=(P(dp, None), P(dp, None)),
        check_vma=False,
    )
```
